1024 devices in a mesh: dp: 32 (over x, y, core), tensor: 32 (over z).
Axes of the slice: x: 4, y: 4, z: 32, core: 2. Of those that a mesh axis runs over, the one named last changes fastest.
Arguments:
- gradients: float32 [32, 128, 28672], P('dp', None, 'tensor'), may hold values from -110 to 110
- error_memory: bfloat16 [32, 128, 28672], P('dp', None, 'tensor'), may hold values from -2 to 2
- q_start: float32 [28672, 32], P('tensor'), may hold values from -5 to 5
Outputs:
- p_factor: float32 [128, 32], P('tensor')
- q_factor: float32 [28672, 32], P('tensor')
- new_error: bfloat16 [32, 128, 28672], P('dp', None, 'tensor')
The draws below stay inside these ranges and needn't reach their ends.
All inputs are finite; a program needn't handle non-finite values.
Results may differ from the reference program's by a relative error of at most 0.0019.
Values sent between devices are 32-bit elements; how exact they have to be, the bound alone decides.
A program may use at most 32 MiB of HBM per device.

```python
import math
import jax
import jax.numpy as jnp
from jax import lax

ROWS = 128
RANK = 32
ITERS = 2
COLS = 28672
REPLICAS = 32


def draw_gradients(key, part):
    key = jax.random.fold_in(key, 11)
    keys = jax.random.split(key, 5)
    common = jnp.clip(jax.random.normal(keys[0], (ROWS, COLS), jnp.float32), -5.0, 5.0)
    noise = jnp.clip(jax.random.normal(keys[1], (REPLICAS, ROWS, COLS), jnp.float32), -5.0, 5.0)
    row_scale = jnp.exp(jax.random.uniform(keys[2], (1, ROWS, 1), jnp.float32, math.log(0.3), math.log(3.0)))
    col_scale = jnp.exp(jax.random.uniform(keys[3], (1, 1, COLS), jnp.float32, math.log(0.3), math.log(3.0)))
    rep_scale = jnp.exp(jax.random.uniform(keys[4], (REPLICAS, 1, 1), jnp.float32, math.log(0.5), math.log(1.5)))
    mixed = 0.8 * common[None] + rep_scale * noise
    return (row_scale * col_scale * mixed).astype(jnp.float32)


def block_scale(rng, dims, pieces, low, largest):
    level = 1.0
    for axis_at, parts in pieces:
        draws = jax.random.uniform(jax.random.fold_in(jax.random.fold_in(rng, 6), axis_at), (parts,), jnp.float32, low / len(pieces), largest / len(pieces))
        level = level * jnp.repeat(jnp.exp(draws), dims[axis_at] // parts).reshape((-1,) + (1,) * (len(dims) - 1 - axis_at))
    return level


def normal_values(stream_key, extent, spread, reach, cuts=(), dtype=jnp.bfloat16):
    values = spread * jax.random.normal(stream_key, extent, jnp.float32)
    if cuts:
        values = values * block_scale(stream_key, extent, cuts, -0.22, 0.18)
    return jnp.clip(values, -reach, reach).astype(dtype)


def setup_inputs(seed: int = 0) -> dict:
    streams_of = jax.random.split(jax.random.key(seed), 4)
    gradients = draw_gradients(jax.random.fold_in(streams_of[3], 71), 0)
    error_memory = normal_values(streams_of[1], (REPLICAS, ROWS, COLS), 0.3, 2.0, ((0, 32), (2, 32)))
    q_start = normal_values(streams_of[2], (COLS, RANK), 1.0, 5.0, ((0, 32),), jnp.float32)
    return {"gradients": gradients, "error_memory": error_memory, "q_start": q_start}


def orthonormal(p_sum):
    gram = jnp.dot(p_sum.T, p_sum, precision=lax.Precision.HIGHEST)
    chol = jnp.linalg.cholesky(gram)
    return jax.scipy.linalg.solve_triangular(chol, p_sum.T, lower=True).T

def reference(gradients, error_memory, q_start):

    def corrected(index):
        return gradients[index] + error_memory[index].astype(jnp.float32)
    indices = jnp.arange(REPLICAS).astype(jnp.int32)
    q_now = q_start
    p_orth = jnp.zeros((ROWS, RANK), jnp.float32)
    for step in range(ITERS):

        def add_left(total, index):
            return (total + jnp.dot(corrected(index), q_now, precision=lax.Precision.HIGHEST), None)
        p_sum, unused = lax.scan(add_left, jnp.zeros((ROWS, RANK), jnp.float32), indices)
        p_orth = orthonormal(p_sum)

        def add_right(total, index):
            return (total + jnp.dot(corrected(index).T, p_orth, precision=lax.Precision.HIGHEST), None)
        q_sum, unused = lax.scan(add_right, jnp.zeros((COLS, RANK), jnp.float32), indices)
        q_now = q_sum / REPLICAS
    product = jnp.dot(p_orth, q_now.T, precision=lax.Precision.HIGHEST)
    new_error = lax.map(lambda index: (corrected(index) - product).astype(jnp.bfloat16), indices)
    return (p_orth, q_now, new_error)
```

```python
import jax
import jax.numpy as jnp
from jax import lax
from jax.experimental import pallas as pl
from jax.experimental.pallas import tpu as pltpu
from jax.sharding import PartitionSpec as P

MESH = pl.DeviceIdType.MESH
HIGH = lax.Precision.HIGHEST
ROWS = 128
COLS = 896
HALF = 448
RANK = 32
CHIPS = 16
OWNERS = 14
SLICE = 32
SOURCES = 2 * OWNERS
DEPTH = 32
PLANE = 32


def dot(left, right, left_dim, right_dim):
    return lax.dot_general(
        left,
        right,
        (((left_dim,), (right_dim,)), ((), ())),
        precision=HIGH,
        preferred_element_type=jnp.float32,
    )


def wait_bytes(ref, sem):
    pltpu.make_async_copy(ref, ref, sem).wait()


def reduce_kernel(
    g_hbm, e_hbm, q_hbm, m_out, st_out,
    g_v, e_v, q_v, ct, sib, rs, part, tiles, zb,
    load_sem, sib_sem, rs_sem, tile_sem, z_sem, m_sem, st_sem, go_sem,
):
    dp = lax.axis_index("dp")
    z = lax.axis_index("tensor")
    core = lax.rem(dp, 2)
    chip = lax.div(dp, 2)

    loads = [
        pltpu.make_async_copy(g_hbm.at[0], g_v, load_sem.at[0]),
        pltpu.make_async_copy(e_hbm.at[0], e_v, load_sem.at[1]),
        pltpu.make_async_copy(q_hbm, q_v, load_sem.at[2]),
    ]
    for load in loads:
        load.start()

    barrier = pltpu.get_barrier_semaphore()

    @pl.loop(0, CHIPS)
    def _(j):
        @pl.when(2 * j != dp)
        def _():
            pl.semaphore_signal(barrier, inc=1, device_id=(2 * j, z), device_id_type=MESH)

    @pl.when(core == 1)
    def _():
        @pl.loop(1, DEPTH)
        def _(k):
            pl.semaphore_signal(
                barrier, inc=1, device_id=(dp, lax.rem(z + k, DEPTH)), device_id_type=MESH
            )

    for load in loads:
        load.wait()
    for b in range(COLS // 128):
        cols = slice(128 * b, 128 * b + 128)
        ct[cols, :] = (g_v[:, cols] + e_v[:, cols].astype(jnp.float32)).T

    @pl.when(core == 0)
    def _():
        pl.semaphore_wait(barrier, PLANE - 1)
        pl.semaphore_signal(go_sem, inc=1, device_id=(dp + 1, z), device_id_type=MESH)

    @pl.when(core == 1)
    def _():
        pl.semaphore_wait(go_sem, 1)

    mine = pl.multiple_of(core * HALF, 8)
    other = pl.multiple_of((1 - core) * HALF, 8)
    swap = pltpu.make_async_remote_copy(
        src_ref=ct.at[pl.ds(other, HALF)], dst_ref=sib, send_sem=sib_sem.at[0], recv_sem=sib_sem.at[1],
        device_id=(dp + 1 - 2 * core, z), device_id_type=MESH,
    )
    swap.start()
    swap.wait_recv()
    ct[pl.ds(mine, HALF), :] += sib[...]

    @pl.loop(0, OWNERS)
    def _(j):
        @pl.when(j != chip)
        def _():
            pltpu.make_async_remote_copy(
                src_ref=ct.at[pl.ds(pl.multiple_of(mine + SLICE * j, 8), SLICE)], dst_ref=rs.at[chip],
                send_sem=rs_sem.at[0], recv_sem=rs_sem.at[1],
                device_id=(2 * j + core, z), device_id_type=MESH,
            ).start()

    own = pl.multiple_of(mine + SLICE * lax.min(chip, OWNERS - 1), 8)
    source = core * OWNERS + lax.min(chip, OWNERS - 1)

    @pl.when(chip < OWNERS)
    def _():
        rs[chip] = ct[pl.ds(own, SLICE), :]
        wait_bytes(rs.at[pl.ds(0, CHIPS - 1)], rs_sem.at[1])
        total = rs[0]
        for j in range(1, CHIPS):
            total += rs[j]
        st_out[pl.ds(own, SLICE), :] = total
        gram = dot(total, total, 0, 0)
        left = dot(q_v[pl.ds(own, SLICE), :], total, 0, 0)
        for t in range(4):
            part[t] = left[8 * t : 8 * t + 8]
        for t in range(8):
            part[4 + t] = gram[8 * t : 8 * t + 8]
        upper = gram[64:96, :]
        lower = pltpu.roll(gram[96:128, :], 64, 1)
        lane = lax.broadcasted_iota(jnp.int32, (32, 128), 1)
        packed = jnp.where(lane < 64, lower, upper)
        for t in range(4):
            part[12 + t] = packed[8 * t : 8 * t + 8]

        @pl.loop(0, CHIPS)
        def _(j):
            @pl.when(2 * j + 1 != dp)
            def _():
                pltpu.make_async_remote_copy(
                    src_ref=part.at[j], dst_ref=tiles.at[source], send_sem=tile_sem.at[0], recv_sem=tile_sem.at[1],
                    device_id=(2 * j + 1, z), device_id_type=MESH,
                ).start()

    @pl.when(core == 1)
    def _():
        @pl.when(chip < OWNERS)
        def _():
            tiles[source] = part[chip]
            wait_bytes(tiles.at[pl.ds(0, SOURCES - 1)], tile_sem.at[1])

        @pl.when(chip >= OWNERS)
        def _():
            wait_bytes(tiles, tile_sem.at[1])

        total = tiles[0]
        for j in range(1, SOURCES):
            total += tiles[j]
        zb[z] = total
        pl.semaphore_wait(barrier, DEPTH - 1)

        @pl.loop(0, DEPTH - 1)
        def _(k):
            half = lax.div(k + 1, 2)
            shift = jnp.where(lax.rem(k, 2) == 0, 16 + half, 16 - half)
            pltpu.make_async_remote_copy(
                src_ref=zb.at[z], dst_ref=zb.at[z], send_sem=z_sem.at[0], recv_sem=z_sem.at[1],
                device_id=(dp, lax.rem(z + shift, DEPTH)), device_id_type=MESH,
            ).start()

    @pl.when(chip < OWNERS)
    def _():
        @pl.loop(1, PLANE)
        def _(k):
            pltpu.make_async_remote_copy(
                src_ref=st_out.at[pl.ds(own, SLICE)], dst_ref=st_out.at[pl.ds(own, SLICE)],
                send_sem=st_sem.at[0], recv_sem=st_sem.at[1],
                device_id=(lax.rem(dp + k, PLANE), z), device_id_type=MESH,
            ).start()

    @pl.when(core == 1)
    def _():
        wait_bytes(zb.at[pl.ds(0, DEPTH - 1)], z_sem.at[1])
        total = zb[0]
        for j in range(1, DEPTH):
            total += zb[j]
        m_out[chip] = total

        @pl.loop(1, PLANE)
        def _(k):
            pltpu.make_async_remote_copy(
                src_ref=m_out.at[chip], dst_ref=m_out.at[chip], send_sem=m_sem.at[0], recv_sem=m_sem.at[1],
                device_id=(lax.rem(dp + k, PLANE), z), device_id_type=MESH,
            ).start()
        wait_bytes(m_out.at[pl.ds(0, CHIPS - 1)], m_sem.at[1])
        wait_bytes(zb.at[pl.ds(0, DEPTH - 1)], z_sem.at[0])
        wait_bytes(zb.at[pl.ds(0, PLANE - 1)], m_sem.at[0])

    @pl.when(core == 0)
    def _():
        wait_bytes(m_out, m_sem.at[1])

    swap.wait_send()

    @pl.when(chip < OWNERS)
    def _():
        wait_bytes(st_out.at[pl.ds(0, COLS - SLICE)], st_sem.at[1])
        wait_bytes(ct.at[pl.ds(0, SLICE * (OWNERS - 1))], rs_sem.at[0])
        wait_bytes(st_out, st_sem.at[0])
        wait_bytes(st_out.at[pl.ds(0, COLS // 28 * 3)], st_sem.at[0])

        @pl.when(core == 0)
        def _():
            wait_bytes(part, tile_sem.at[0])

        @pl.when(core == 1)
        def _():
            wait_bytes(part.at[pl.ds(0, CHIPS - 1)], tile_sem.at[0])

    @pl.when(chip >= OWNERS)
    def _():
        wait_bytes(st_out, st_sem.at[1])
        wait_bytes(ct.at[pl.ds(0, HALF)], rs_sem.at[0])


def reduce_call(gradients, error_memory, q_start):
    any_space = pl.BlockSpec(memory_space=pl.ANY)
    vmem = pl.BlockSpec(memory_space=pltpu.VMEM)
    pair = pltpu.SemaphoreType.DMA((2,))
    return pl.pallas_call(
        reduce_kernel,
        out_shape=(
            jax.ShapeDtypeStruct((CHIPS, 8, 128), jnp.float32),
            jax.ShapeDtypeStruct((COLS, ROWS), jnp.float32),
        ),
        in_specs=[any_space] * 3,
        out_specs=(vmem, vmem),
        scratch_shapes=[
            pltpu.VMEM((ROWS, COLS), jnp.float32),
            pltpu.VMEM((ROWS, COLS), jnp.bfloat16),
            pltpu.VMEM((COLS, RANK), jnp.float32),
            pltpu.VMEM((COLS, ROWS), jnp.float32),
            pltpu.VMEM((HALF, ROWS), jnp.float32),
            pltpu.VMEM((CHIPS, SLICE, ROWS), jnp.float32),
            pltpu.VMEM((CHIPS, 8, 128), jnp.float32),
            pltpu.VMEM((SOURCES, 8, 128), jnp.float32),
            pltpu.VMEM((DEPTH, 8, 128), jnp.float32),
            pltpu.SemaphoreType.DMA((3,)),
            pair, pair, pair, pair, pair, pair,
            pltpu.SemaphoreType.REGULAR,
        ],
        compiler_params=pltpu.CompilerParams(
            collective_id=0, has_side_effects=True, vmem_limit_bytes=16 << 20
        ),
        name="plane_and_line_sums",
    )(gradients, error_memory, q_start)


def orthonormal_rows(pt):
    gram = dot(pt, pt, 1, 1)
    row = lax.broadcasted_iota(jnp.int32, (RANK, 1), 0)
    for k in range(RANK):
        pivot = gram[k : k + 1, k : k + 1]
        factor = jnp.where(row > k, gram[:, k : k + 1] / pivot, 0.0)
        gram, pt = gram - factor * gram[k : k + 1, :], pt - factor * pt[k : k + 1, :]
    diag = lax.broadcasted_iota(jnp.int32, (RANK, RANK), 0) == lax.broadcasted_iota(jnp.int32, (RANK, RANK), 1)
    pivots = jnp.sum(jnp.where(diag, gram, 0.0), axis=1, keepdims=True)
    return pt / jnp.sqrt(pivots)


def factor_kernel(m_ref, st_ref, g_hbm, e_hbm, p_out, q_out, new_out, g_v, e_v, load_sem):
    loads = [
        pltpu.make_async_copy(g_hbm.at[0], g_v, load_sem.at[0]),
        pltpu.make_async_copy(e_hbm.at[0], e_v, load_sem.at[1]),
    ]
    for load in loads:
        load.start()
    pt = jnp.concatenate([m_ref[t] for t in range(4)], axis=0)
    top = jnp.concatenate([m_ref[4 + t] for t in range(8)], axis=0)
    packed = jnp.concatenate([m_ref[12 + t] for t in range(4)], axis=0)
    lane = lax.broadcasted_iota(jnp.int32, (64, 128), 1)
    right = jnp.concatenate([packed, pltpu.roll(packed, 64, 1)], axis=0)
    wide = jnp.concatenate([top, top], axis=0).T
    bottom = jnp.where(lane < 64, wide[64:128, :], right)
    gram = jnp.concatenate([top, bottom], axis=0)

    first = orthonormal_rows(pt)
    second = dot(first, gram, 1, 0) * (1.0 / REPLICAS)
    pt = orthonormal_rows(second)

    z = lax.axis_index("tensor")
    pick = lax.broadcasted_iota(jnp.int32, (8, ROWS), 0) + 4 * z == lax.broadcasted_iota(jnp.int32, (8, ROWS), 1)
    p_out[...] = dot(pick.astype(jnp.float32), pt, 1, 1)[0:4, :]
    st = st_ref[...]
    q_out[...] = dot(st, pt, 1, 1) * (1.0 / REPLICAS)
    qt = dot(pt, st, 1, 1) * (1.0 / REPLICAS)
    product = dot(pt, qt, 0, 0)
    for load in loads:
        load.wait()
    new_out[0] = (g_v[...] + e_v[...].astype(jnp.float32) - product).astype(jnp.bfloat16)


REPLICAS = 32


def factor_call(tiles, st, gradients, error_memory):
    any_space = pl.BlockSpec(memory_space=pl.ANY)
    vmem = pl.BlockSpec(memory_space=pltpu.VMEM)
    return pl.pallas_call(
        factor_kernel,
        out_shape=(
            jax.ShapeDtypeStruct((4, RANK), jnp.float32),
            jax.ShapeDtypeStruct((COLS, RANK), jnp.float32),
            jax.ShapeDtypeStruct((1, ROWS, COLS), jnp.bfloat16),
        ),
        in_specs=[vmem, vmem, any_space, any_space],
        out_specs=(vmem, vmem, vmem),
        scratch_shapes=[
            pltpu.VMEM((ROWS, COLS), jnp.float32),
            pltpu.VMEM((ROWS, COLS), jnp.bfloat16),
            pltpu.SemaphoreType.DMA((2,)),
        ],
        compiler_params=pltpu.CompilerParams(vmem_limit_bytes=16 << 20),
        name="factors",
    )(tiles, st, gradients, error_memory)


def local(gradients, error_memory, q_start):
    tiles, st = reduce_call(gradients, error_memory, q_start)
    return factor_call(tiles, st, gradients, error_memory)


def solution(mesh):
    in_specs = (P("dp", None, "tensor"), P("dp", None, "tensor"), P("tensor", None))
    out_specs = (P("tensor", None), P("tensor", None), P("dp", None, "tensor"))
    return jax.shard_map(local, mesh=mesh, in_specs=in_specs, out_specs=out_specs, check_vma=False)
```

```python
import jax
import jax.numpy as jnp
from jax import lax
from jax.experimental import pallas as pl
from jax.experimental.pallas import tpu as pltpu
from jax.sharding import PartitionSpec as P

MESH = pl.DeviceIdType.MESH
HIGH = lax.Precision.HIGHEST
ROWS = 128
COLS = 896
HALF = 448
RANK = 32
CHIPS = 16
OWNERS = 14
SLICE = 32
SOURCES = 2 * OWNERS
DEPTH = 32
PLANE = 32
REPLICAS = 32
BLOCK = 16
VMEM_LIMIT = (64 << 20) - (1100 << 10)


def dot(left, right, left_dim, right_dim):
    return lax.dot_general(
        left,
        right,
        (((left_dim,), (right_dim,)), ((), ())),
        precision=HIGH,
        preferred_element_type=jnp.float32,
    )


def wait_bytes(ref, sem):
    pltpu.make_async_copy(ref, ref, sem).wait()


def reduce_kernel(
    g_hbm, e_hbm, qt_hbm, m_out, st_out, c_out,
    g_v, e_v, qt_v, q_v, ct, sib, rs, part, tiles, zb,
    load_sem, sib_sem, rs_sem, tile_sem, z_sem, m_sem, st_sem, go_sem,
):
    dp = lax.axis_index("dp")
    z = lax.axis_index("tensor")
    core = lax.rem(dp, 2)
    chip = lax.div(dp, 2)

    loads = [
        pltpu.make_async_copy(g_hbm.at[0], g_v, load_sem.at[0]),
        pltpu.make_async_copy(e_hbm.at[0], e_v, load_sem.at[1]),
        pltpu.make_async_copy(qt_hbm, qt_v, load_sem.at[2]),
    ]
    for load in loads:
        load.start()

    barrier = pltpu.get_barrier_semaphore()

    @pl.loop(0, CHIPS)
    def _(j):
        @pl.when(2 * j != dp)
        def _():
            pl.semaphore_signal(barrier, inc=1, device_id=(2 * j, z), device_id_type=MESH)

    @pl.when(core == 1)
    def _():
        @pl.loop(1, DEPTH)
        def _(k):
            pl.semaphore_signal(
                barrier, inc=1, device_id=(dp, lax.rem(z + k, DEPTH)), device_id_type=MESH
            )

    for load in loads:
        load.wait()
    for b in range(COLS // 128):
        cols = slice(128 * b, 128 * b + 128)
        corrected = g_v[:, cols] + e_v[:, cols].astype(jnp.float32)
        c_out[:, cols] = corrected
        ct[cols, :] = corrected.T
        q_v[cols, :] = qt_v[:, cols].T

    @pl.when(core == 0)
    def _():
        pl.semaphore_wait(barrier, PLANE - 1)
        pl.semaphore_signal(go_sem, inc=1, device_id=(dp + 1, z), device_id_type=MESH)

    @pl.when(core == 1)
    def _():
        pl.semaphore_wait(go_sem, 1)

    mine = pl.multiple_of(core * HALF, 8)
    other = pl.multiple_of((1 - core) * HALF, 8)
    swap = pltpu.make_async_remote_copy(
        src_ref=ct.at[pl.ds(other, HALF)], dst_ref=sib, send_sem=sib_sem.at[0], recv_sem=sib_sem.at[1],
        device_id=(dp + 1 - 2 * core, z), device_id_type=MESH,
    )
    swap.start()
    swap.wait_recv()
    ct[pl.ds(mine, HALF), :] += sib[...]

    @pl.loop(0, OWNERS)
    def _(j):
        @pl.when(j != chip)
        def _():
            pltpu.make_async_remote_copy(
                src_ref=ct.at[pl.ds(pl.multiple_of(mine + SLICE * j, 8), SLICE)], dst_ref=rs.at[chip],
                send_sem=rs_sem.at[0], recv_sem=rs_sem.at[1],
                device_id=(2 * j + core, z), device_id_type=MESH,
            ).start()

    own = pl.multiple_of(mine + SLICE * lax.min(chip, OWNERS - 1), 8)
    source = core * OWNERS + lax.min(chip, OWNERS - 1)

    @pl.when(chip < OWNERS)
    def _():
        rs[chip] = ct[pl.ds(own, SLICE), :]
        wait_bytes(rs.at[pl.ds(0, CHIPS - 1)], rs_sem.at[1])
        total = rs[0]
        for j in range(1, CHIPS):
            total += rs[j]
        st_out[pl.ds(own, SLICE), :] = total
        gram = dot(total, total, 0, 0)
        left = dot(q_v[pl.ds(own, SLICE), :], total, 0, 0)
        for t in range(4):
            part[t] = left[8 * t : 8 * t + 8]
        for t in range(8):
            part[4 + t] = gram[8 * t : 8 * t + 8]
        upper = gram[64:96, :]
        lower = pltpu.roll(gram[96:128, :], 64, 1)
        lane = lax.broadcasted_iota(jnp.int32, (32, 128), 1)
        packed = jnp.where(lane < 64, lower, upper)
        for t in range(4):
            part[12 + t] = packed[8 * t : 8 * t + 8]

        @pl.loop(0, CHIPS)
        def _(j):
            @pl.when(2 * j + 1 != dp)
            def _():
                pltpu.make_async_remote_copy(
                    src_ref=part.at[j], dst_ref=tiles.at[source], send_sem=tile_sem.at[0], recv_sem=tile_sem.at[1],
                    device_id=(2 * j + 1, z), device_id_type=MESH,
                ).start()

    @pl.when(core == 1)
    def _():
        @pl.when(chip < OWNERS)
        def _():
            tiles[source] = part[chip]
            wait_bytes(tiles.at[pl.ds(0, SOURCES - 1)], tile_sem.at[1])

        @pl.when(chip >= OWNERS)
        def _():
            wait_bytes(tiles, tile_sem.at[1])

        total = tiles[0]
        for j in range(1, SOURCES):
            total += tiles[j]
        zb[z] = total
        pl.semaphore_wait(barrier, DEPTH - 1)

        @pl.loop(0, DEPTH - 1)
        def _(k):
            half = lax.div(k + 1, 2)
            shift = jnp.where(lax.rem(k, 2) == 0, 16 + half, 16 - half)
            pltpu.make_async_remote_copy(
                src_ref=zb.at[z], dst_ref=zb.at[z], send_sem=z_sem.at[0], recv_sem=z_sem.at[1],
                device_id=(dp, lax.rem(z + shift, DEPTH)), device_id_type=MESH,
            ).start()

    @pl.when(chip < OWNERS)
    def _():
        @pl.loop(1, PLANE)
        def _(k):
            pltpu.make_async_remote_copy(
                src_ref=st_out.at[pl.ds(own, SLICE)], dst_ref=st_out.at[pl.ds(own, SLICE)],
                send_sem=st_sem.at[0], recv_sem=st_sem.at[1],
                device_id=(lax.rem(dp + k, PLANE), z), device_id_type=MESH,
            ).start()

    @pl.when(chip < OWNERS)
    def _():
        wait_bytes(st_out.at[pl.ds(0, COLS - SLICE)], st_sem.at[1])

    @pl.when(chip >= OWNERS)
    def _():
        wait_bytes(st_out, st_sem.at[1])

    @pl.when(core == 1)
    def _():
        wait_bytes(zb.at[pl.ds(0, DEPTH - 1)], z_sem.at[1])
        total = zb[0]
        for j in range(1, DEPTH):
            total += zb[j]
        m_out[chip] = total

        @pl.loop(1, PLANE)
        def _(k):
            pltpu.make_async_remote_copy(
                src_ref=m_out.at[chip], dst_ref=m_out.at[chip], send_sem=m_sem.at[0], recv_sem=m_sem.at[1],
                device_id=(lax.rem(dp + k, PLANE), z), device_id_type=MESH,
            ).start()
        wait_bytes(m_out.at[pl.ds(0, CHIPS - 1)], m_sem.at[1])
        wait_bytes(zb.at[pl.ds(0, DEPTH - 1)], z_sem.at[0])
        wait_bytes(zb.at[pl.ds(0, PLANE - 1)], m_sem.at[0])

    @pl.when(core == 0)
    def _():
        wait_bytes(m_out, m_sem.at[1])

    swap.wait_send()

    @pl.when(chip < OWNERS)
    def _():
        wait_bytes(ct.at[pl.ds(0, SLICE * (OWNERS - 1))], rs_sem.at[0])
        wait_bytes(st_out, st_sem.at[0])
        wait_bytes(st_out.at[pl.ds(0, COLS // 28 * 3)], st_sem.at[0])

        @pl.when(core == 0)
        def _():
            wait_bytes(part, tile_sem.at[0])

        @pl.when(core == 1)
        def _():
            wait_bytes(part.at[pl.ds(0, CHIPS - 1)], tile_sem.at[0])

    @pl.when(chip >= OWNERS)
    def _():
        wait_bytes(ct.at[pl.ds(0, HALF)], rs_sem.at[0])


def reduce_call(gradients, error_memory, qt_start):
    hbm = pl.BlockSpec(memory_space=pltpu.HBM)
    vmem = pl.BlockSpec(memory_space=pltpu.VMEM)
    pair = pltpu.SemaphoreType.DMA((2,))
    return pl.pallas_call(
        reduce_kernel,
        out_shape=(
            pltpu.VMEM((CHIPS, 8, 128), jnp.float32),
            pltpu.VMEM((COLS, ROWS), jnp.float32),
            pltpu.VMEM((ROWS, COLS), jnp.float32),
        ),
        in_specs=[hbm] * 3,
        out_specs=(vmem, vmem, vmem),
        scratch_shapes=[
            pltpu.VMEM((ROWS, COLS), jnp.float32),
            pltpu.VMEM((ROWS, COLS), jnp.bfloat16),
            pltpu.VMEM((RANK, COLS), jnp.float32),
            pltpu.VMEM((COLS, RANK), jnp.float32),
            pltpu.VMEM((COLS, ROWS), jnp.float32),
            pltpu.VMEM((HALF, ROWS), jnp.float32),
            pltpu.VMEM((CHIPS, SLICE, ROWS), jnp.float32),
            pltpu.VMEM((CHIPS, 8, 128), jnp.float32),
            pltpu.VMEM((SOURCES, 8, 128), jnp.float32),
            pltpu.VMEM((DEPTH, 8, 128), jnp.float32),
            pltpu.SemaphoreType.DMA((3,)),
            pair, pair, pair, pair, pair, pair,
            pltpu.SemaphoreType.REGULAR,
        ],
        compiler_params=pltpu.CompilerParams(
            collective_id=0, has_side_effects=True, vmem_limit_bytes=VMEM_LIMIT
        ),
        name="plane_and_line_sums",
    )(gradients, error_memory, qt_start)


def orthonormal_rows(pt):
    gram = dot(pt, pt, 1, 1)
    high = RANK // 8
    gram = [gram[8 * t : 8 * t + 8] for t in range(high)]
    rows = [pt[8 * t : 8 * t + 8] for t in range(high)]
    pivots = [jnp.ones((8, ROWS), jnp.float32) for t in range(high)]
    sub = lax.broadcasted_iota(jnp.int32, (8, ROWS), 0)
    for first in range(0, RANK, BLOCK):
        more = first + BLOCK < RANK
        cols = [
            [jnp.broadcast_to(gram[t][:, first + j : first + j + 1], (8, ROWS)) for t in range(high)]
            for j in range(BLOCK)
        ]
        for j in range(BLOCK):
            at, s = divmod(first + j, 8)
            pivot = jnp.broadcast_to(cols[j][at][s : s + 1], (8, ROWS))
            inverse = 1.0 / pivot
            factor = [None] * high
            for t in range(at, high):
                factor[t] = cols[j][t] * inverse
            factor[at] = jnp.where(sub > s, factor[at], 0.0)
            for later in range(j + 1, BLOCK):
                entry = jnp.broadcast_to(cols[later][at][s : s + 1], (8, ROWS))
                for t in range(at, high):
                    cols[later][t] = cols[later][t] - factor[t] * entry
            row = jnp.broadcast_to(rows[at][s : s + 1], (8, ROWS))
            for t in range(at, high):
                rows[t] = rows[t] - factor[t] * row
            if more:
                line = jnp.broadcast_to(gram[at][s : s + 1], (8, RANK))
                for t in range(at, high):
                    gram[t] = gram[t] - factor[t][:, :RANK] * line
            pivots[at] = jnp.where(sub == s, pivot, pivots[at])
    return jnp.concatenate([rows[t] / jnp.sqrt(pivots[t]) for t in range(high)], axis=0)


def factor_kernel(m_ref, st_ref, c_ref, p_out, qt_out, new_hbm, new_v, store_sem):
    pt = jnp.concatenate([m_ref[t] for t in range(4)], axis=0)
    top = jnp.concatenate([m_ref[4 + t] for t in range(8)], axis=0)
    packed = jnp.concatenate([m_ref[12 + t] for t in range(4)], axis=0)
    lane = lax.broadcasted_iota(jnp.int32, (64, 128), 1)
    right = jnp.concatenate([packed, pltpu.roll(packed, 64, 1)], axis=0)
    wide = jnp.concatenate([top, top], axis=0).T
    bottom = jnp.where(lane < 64, wide[64:128, :], right)
    gram = jnp.concatenate([top, bottom], axis=0)

    first = orthonormal_rows(pt)
    second = dot(first, gram, 1, 0) * (1.0 / REPLICAS)
    pt = orthonormal_rows(second)

    z = lax.axis_index("tensor")
    pick = lax.broadcasted_iota(jnp.int32, (8, ROWS), 0) + 4 * z == lax.broadcasted_iota(jnp.int32, (8, ROWS), 1)
    p_out[...] = dot(pick.astype(jnp.float32), pt, 1, 1)[0:4, :]
    scaled = pt * (1.0 / REPLICAS)
    copies = []
    for b in range(COLS // 128):
        cols = slice(128 * b, 128 * b + 128)
        q = dot(st_ref[cols, :], scaled, 1, 1)
        qt_out[:, cols] = q.T
        new_v[:, cols] = (c_ref[:, cols] - dot(q, pt, 1, 0).T).astype(jnp.bfloat16)
        copies.append(pltpu.make_async_copy(new_v.at[:, cols], new_hbm.at[0, :, cols], store_sem.at[b]))
        copies[b].start()
    for copy in copies:
        copy.wait()


def factor_call(tiles, st, corrected):
    hbm = pl.BlockSpec(memory_space=pltpu.HBM)
    vmem = pl.BlockSpec(memory_space=pltpu.VMEM)
    return pl.pallas_call(
        factor_kernel,
        out_shape=(
            jax.ShapeDtypeStruct((4, RANK), jnp.float32),
            jax.ShapeDtypeStruct((RANK, COLS), jnp.float32),
            jax.ShapeDtypeStruct((1, ROWS, COLS), jnp.bfloat16),
        ),
        in_specs=[vmem, vmem, vmem],
        out_specs=(vmem, vmem, hbm),
        scratch_shapes=[
            pltpu.VMEM((ROWS, COLS), jnp.bfloat16),
            pltpu.SemaphoreType.DMA((COLS // 128,)),
        ],
        compiler_params=pltpu.CompilerParams(vmem_limit_bytes=32 << 20),
        name="factors",
    )(tiles, st, corrected)


def local(gradients, error_memory, q_start):
    tiles, st, corrected = reduce_call(gradients, error_memory, q_start.T)
    p_rows, qt, new_error = factor_call(tiles, st, corrected)
    return p_rows, qt.T, new_error


def solution(mesh):
    in_specs = (P("dp", None, "tensor"), P("dp", None, "tensor"), P("tensor", None))
    out_specs = (P("tensor", None), P("tensor", None), P("dp", None, "tensor"))
    return jax.shard_map(local, mesh=mesh, in_specs=in_specs, out_specs=out_specs, check_vma=False)
```

```python
import jax
import jax.numpy as jnp
from jax import lax
from jax.experimental import pallas as pl
from jax.experimental.pallas import tpu as pltpu
from jax.sharding import PartitionSpec as P

MESH = pl.DeviceIdType.MESH
SIDE = 4
OFFSETS = sorted(
    ((dx, dy) for dx in range(SIDE) for dy in range(SIDE) if dx or dy),
    key=lambda d: -(min(d[0], SIDE - d[0]) + min(d[1], SIDE - d[1])),
)
HIGH = lax.Precision.HIGHEST
ROWS = 128
COLS = 896
HALF = 448
RANK = 32
CHIPS = 16
OWNERS = 14
SLICE = 32
SOURCES = 2 * OWNERS
DEPTH = 32
PLANE = 32
REPLICAS = 32
BLOCK = 16
STEPS = (0, 256, 512, 896)
VMEM_LIMIT = (64 << 20) - (1100 << 10)


def dot(left, right, left_dim, right_dim):
    return lax.dot_general(
        left,
        right,
        (((left_dim,), (right_dim,)), ((), ())),
        precision=HIGH,
        preferred_element_type=jnp.float32,
    )


def halves(value):
    high = value.astype(jnp.bfloat16)
    return high, (value - high.astype(jnp.float32)).astype(jnp.bfloat16)


def wait_bytes(ref, sem):
    pltpu.make_async_copy(ref, ref, sem).wait()


def shifted(chip, offset):
    x, y = lax.div(chip, SIDE), lax.rem(chip, SIDE)
    return SIDE * lax.rem(x + offset[0], SIDE) + lax.rem(y + offset[1], SIDE)


def reduce_kernel(
    g_hbm, e_hbm, qt_hbm, m_out, s_out, c_out,
    g_v, e_v, qt_v, q_v, ct, sib, rs, part, tiles, zb, st_v,
    load_sem, sib_sem, rs_sem, tile_sem, z_sem, m_sem, st_sem, go_sem, later_sem,
):
    dp = lax.axis_index("dp")
    z = lax.axis_index("tensor")
    core = lax.rem(dp, 2)
    chip = lax.div(dp, 2)

    loads = [
        pltpu.make_async_copy(g_hbm.at[0], g_v, load_sem.at[0]),
        pltpu.make_async_copy(e_hbm.at[0], e_v, load_sem.at[1]),
        pltpu.make_async_copy(qt_hbm, qt_v, load_sem.at[2]),
    ]
    for load in loads:
        load.start()

    barrier = pltpu.get_barrier_semaphore()

    @pl.loop(0, CHIPS)
    def _(j):
        @pl.when(2 * j != dp)
        def _():
            pl.semaphore_signal(barrier, inc=1, device_id=(2 * j, z), device_id_type=MESH)

    @pl.when(core == 1)
    def _():
        @pl.loop(1, DEPTH)
        def _(k):
            pl.semaphore_signal(
                barrier, inc=1, device_id=(dp, lax.rem(z + k, DEPTH)), device_id_type=MESH
            )

    for load in loads:
        load.wait()
    for b in range(COLS // 128):
        cols = slice(128 * b, 128 * b + 128)
        corrected = g_v[:, cols] + e_v[:, cols].astype(jnp.float32)
        c_out[:, cols] = corrected
        ct[cols, :] = corrected.T
        q_v[cols, :] = qt_v[:, cols].T

    @pl.when(core == 0)
    def _():
        pl.semaphore_wait(barrier, PLANE - 1)
        pl.semaphore_signal(go_sem, inc=1, device_id=(dp + 1, z), device_id_type=MESH)

    @pl.when(core == 1)
    def _():
        pl.semaphore_wait(go_sem, 1)

    mine = pl.multiple_of(core * HALF, 8)
    other = pl.multiple_of((1 - core) * HALF, 8)
    swap = pltpu.make_async_remote_copy(
        src_ref=ct.at[pl.ds(other, HALF)], dst_ref=sib, send_sem=sib_sem.at[0], recv_sem=sib_sem.at[1],
        device_id=(dp + 1 - 2 * core, z), device_id_type=MESH,
    )
    swap.start()
    swap.wait_recv()
    ct[pl.ds(mine, HALF), :] += sib[...]

    for offset in OFFSETS:
        j = shifted(chip, offset)

        @pl.when(j < OWNERS)
        def _():
            pltpu.make_async_remote_copy(
                src_ref=ct.at[pl.ds(pl.multiple_of(mine + SLICE * j, 8), SLICE)], dst_ref=rs.at[chip],
                send_sem=rs_sem.at[0], recv_sem=rs_sem.at[1],
                device_id=(2 * j + core, z), device_id_type=MESH,
            ).start()

    own = pl.multiple_of(mine + SLICE * lax.min(chip, OWNERS - 1), 8)
    source = core * OWNERS + lax.min(chip, OWNERS - 1)

    @pl.when(chip < OWNERS)
    def _():
        rs[chip] = ct[pl.ds(own, SLICE), :]
        wait_bytes(rs.at[pl.ds(0, CHIPS - 1)], rs_sem.at[1])
        total = rs[0]
        for j in range(1, CHIPS):
            total += rs[j]
        st_v[pl.ds(own, SLICE), :] = total
        gram = dot(total, total, 0, 0)
        left = dot(q_v[pl.ds(own, SLICE), :], total, 0, 0)
        for t in range(4):
            part[t] = left[8 * t : 8 * t + 8]
        for t in range(8):
            part[4 + t] = gram[8 * t : 8 * t + 8]
        upper = gram[64:96, :]
        lower = pltpu.roll(gram[96:128, :], 64, 1)
        lane = lax.broadcasted_iota(jnp.int32, (32, 128), 1)
        packed = jnp.where(lane < 64, lower, upper)
        for t in range(4):
            part[12 + t] = packed[8 * t : 8 * t + 8]

        def send_tile(j):
            pltpu.make_async_remote_copy(
                src_ref=part.at[j], dst_ref=tiles.at[source], send_sem=tile_sem.at[0], recv_sem=tile_sem.at[1],
                device_id=(2 * j + 1, z), device_id_type=MESH,
            ).start()

        for offset in OFFSETS:
            send_tile(shifted(chip, offset))

        @pl.when(core == 0)
        def _():
            send_tile(chip)

    @pl.when(core == 1)
    def _():
        @pl.when(chip < OWNERS)
        def _():
            tiles[source] = part[chip]
            wait_bytes(tiles.at[pl.ds(0, SOURCES - 1)], tile_sem.at[1])

        @pl.when(chip >= OWNERS)
        def _():
            wait_bytes(tiles, tile_sem.at[1])

        total = tiles[0]
        for j in range(1, SOURCES):
            total += tiles[j]
        zb[z] = total
        pl.semaphore_wait(barrier, DEPTH - 1)

        @pl.loop(0, DEPTH - 1)
        def _(k):
            half = lax.div(k + 1, 2)
            shift = jnp.where(lax.rem(k, 2) == 0, 16 + half, 16 - half)
            pltpu.make_async_remote_copy(
                src_ref=zb.at[z], dst_ref=zb.at[z], send_sem=z_sem.at[0], recv_sem=z_sem.at[1],
                device_id=(dp, lax.rem(z + shift, DEPTH)), device_id_type=MESH,
            ).start()

        pl.semaphore_signal(later_sem, inc=1, device_id=(dp - 1, z), device_id_type=MESH)

    @pl.when(core == 0)
    def _():
        pl.semaphore_wait(later_sem, 1)

    @pl.when(chip < OWNERS)
    def _():
        @pl.loop(1, PLANE)
        def _(k):
            pltpu.make_async_remote_copy(
                src_ref=st_v.at[pl.ds(own, SLICE)], dst_ref=st_v.at[pl.ds(own, SLICE)],
                send_sem=st_sem.at[0], recv_sem=st_sem.at[1],
                device_id=(lax.rem(dp + k, PLANE), z), device_id_type=MESH,
            ).start()

    @pl.when(chip < OWNERS)
    def _():
        wait_bytes(st_v.at[pl.ds(0, COLS - SLICE)], st_sem.at[1])

    @pl.when(chip >= OWNERS)
    def _():
        wait_bytes(st_v, st_sem.at[1])

    for b in range(COLS // 128):
        cols = slice(128 * b, 128 * b + 128)
        high, low = halves(st_v[cols, :].T)
        s_out[0:ROWS, cols] = high
        s_out[ROWS : 2 * ROWS, cols] = low

    @pl.when(core == 1)
    def _():
        wait_bytes(zb.at[pl.ds(0, DEPTH - 1)], z_sem.at[1])
        total = zb[0]
        for j in range(1, DEPTH):
            total += zb[j]
        m_out[chip] = total

        def send_sum(device):
            pltpu.make_async_remote_copy(
                src_ref=m_out.at[chip], dst_ref=m_out.at[chip], send_sem=m_sem.at[0], recv_sem=m_sem.at[1],
                device_id=(device, z), device_id_type=MESH,
            ).start()

        for offset in OFFSETS:
            j = shifted(chip, offset)
            send_sum(2 * j)
            send_sum(2 * j + 1)
        send_sum(dp - 1)
        wait_bytes(m_out.at[pl.ds(0, CHIPS - 1)], m_sem.at[1])
        wait_bytes(zb.at[pl.ds(0, DEPTH - 1)], z_sem.at[0])
        wait_bytes(zb.at[pl.ds(0, PLANE - 1)], m_sem.at[0])

    @pl.when(core == 0)
    def _():
        wait_bytes(m_out, m_sem.at[1])

    swap.wait_send()

    @pl.when(chip < OWNERS)
    def _():
        wait_bytes(ct.at[pl.ds(0, SLICE * (OWNERS - 1))], rs_sem.at[0])
        wait_bytes(st_v, st_sem.at[0])
        wait_bytes(st_v.at[pl.ds(0, COLS // 28 * 3)], st_sem.at[0])

        @pl.when(core == 0)
        def _():
            wait_bytes(part, tile_sem.at[0])

        @pl.when(core == 1)
        def _():
            wait_bytes(part.at[pl.ds(0, CHIPS - 1)], tile_sem.at[0])

    @pl.when(chip >= OWNERS)
    def _():
        wait_bytes(ct.at[pl.ds(0, HALF)], rs_sem.at[0])


def reduce_call(gradients, error_memory, qt_start):
    hbm = pl.BlockSpec(memory_space=pltpu.HBM)
    vmem = pl.BlockSpec(memory_space=pltpu.VMEM)
    pair = pltpu.SemaphoreType.DMA((2,))
    return pl.pallas_call(
        reduce_kernel,
        out_shape=(
            pltpu.VMEM((CHIPS, 8, 128), jnp.float32),
            pltpu.VMEM((2 * ROWS, COLS), jnp.bfloat16),
            pltpu.VMEM((ROWS, COLS), jnp.float32),
        ),
        in_specs=[hbm] * 3,
        out_specs=(vmem, vmem, vmem),
        scratch_shapes=[
            pltpu.VMEM((ROWS, COLS), jnp.float32),
            pltpu.VMEM((ROWS, COLS), jnp.bfloat16),
            pltpu.VMEM((RANK, COLS), jnp.float32),
            pltpu.VMEM((COLS, RANK), jnp.float32),
            pltpu.VMEM((COLS, ROWS), jnp.float32),
            pltpu.VMEM((HALF, ROWS), jnp.float32),
            pltpu.VMEM((CHIPS, SLICE, ROWS), jnp.float32),
            pltpu.VMEM((CHIPS, 8, 128), jnp.float32),
            pltpu.VMEM((SOURCES, 8, 128), jnp.float32),
            pltpu.VMEM((DEPTH, 8, 128), jnp.float32),
            pltpu.VMEM((COLS, ROWS), jnp.float32),
            pltpu.SemaphoreType.DMA((3,)),
            pair, pair, pair, pair, pair, pair,
            pltpu.SemaphoreType.REGULAR,
            pltpu.SemaphoreType.REGULAR,
        ],
        compiler_params=pltpu.CompilerParams(
            collective_id=0, has_side_effects=True, vmem_limit_bytes=VMEM_LIMIT
        ),
        name="plane_and_line_sums",
    )(gradients, error_memory, qt_start)


def orthonormal_rows(pt):
    gram = dot(pt, pt, 1, 1)
    high = RANK // 8
    gram = [gram[8 * t : 8 * t + 8] for t in range(high)]
    rows = [pt[8 * t : 8 * t + 8] for t in range(high)]
    pivots = [jnp.ones((8, ROWS), jnp.float32) for t in range(high)]
    sub = lax.broadcasted_iota(jnp.int32, (8, ROWS), 0)
    for first in range(0, RANK, BLOCK):
        more = first + BLOCK < RANK
        cols = [
            [jnp.broadcast_to(gram[t][:, first + j : first + j + 1], (8, ROWS)) for t in range(high)]
            for j in range(BLOCK)
        ]
        for j in range(BLOCK):
            at, s = divmod(first + j, 8)
            pivot = jnp.broadcast_to(cols[j][at][s : s + 1], (8, ROWS))
            inverse = 1.0 / pivot
            factor = [None] * high
            for t in range(at, high):
                factor[t] = cols[j][t] * inverse
            factor[at] = jnp.where(sub > s, factor[at], 0.0)
            for later in range(j + 1, BLOCK):
                entry = jnp.broadcast_to(cols[later][at][s : s + 1], (8, ROWS))
                for t in range(at, high):
                    cols[later][t] = cols[later][t] - factor[t] * entry
            row = jnp.broadcast_to(rows[at][s : s + 1], (8, ROWS))
            for t in range(at, high):
                rows[t] = rows[t] - factor[t] * row
            if more:
                line = jnp.broadcast_to(gram[at][s : s + 1], (8, RANK))
                for t in range(at, high):
                    gram[t] = gram[t] - factor[t][:, :RANK] * line
            pivots[at] = jnp.where(sub == s, pivot, pivots[at])
    return jnp.concatenate([rows[t] / jnp.sqrt(pivots[t]) for t in range(high)], axis=0)


def factor_kernel(m_ref, s_ref, c_ref, p_hbm, qt_hbm, new_hbm, p_v, qt_v, new_v, store_sem):
    pt = jnp.concatenate([m_ref[t] for t in range(4)], axis=0)
    top = jnp.concatenate([m_ref[4 + t] for t in range(8)], axis=0)
    packed = jnp.concatenate([m_ref[12 + t] for t in range(4)], axis=0)
    lane = lax.broadcasted_iota(jnp.int32, (64, 128), 1)
    right = jnp.concatenate([packed, pltpu.roll(packed, 64, 1)], axis=0)
    wide = jnp.concatenate([top, top], axis=0).T
    bottom = jnp.where(lane < 64, wide[64:128, :], right)
    gram = jnp.concatenate([top, bottom], axis=0)

    first = orthonormal_rows(pt)
    second = dot(first, gram, 1, 0) * (1.0 / REPLICAS)
    pt = orthonormal_rows(second)

    left = pt.T
    z = lax.axis_index("tensor")
    p_v[0:ROWS, :] = left
    pair = p_v[pl.ds(pl.multiple_of(8 * lax.div(z, 2), 8), 8), :]
    p_v[ROWS : ROWS + 4, :] = jnp.where(lax.rem(z, 2) == 0, pair[0:4], pair[4:8])
    copies = [pltpu.make_async_copy(p_v.at[pl.ds(ROWS, 4)], p_hbm, store_sem.at[0])]
    copies[0].start()

    high, low = halves(pt)
    zero = jnp.zeros_like(low)
    rows = jnp.concatenate(
        [jnp.concatenate([high, high], axis=1), jnp.concatenate([low, zero], axis=1)], axis=0
    )
    high, low = halves(left)
    thrice = jnp.concatenate([high, high, low], axis=1)
    for b in range(len(STEPS) - 1):
        cols = slice(STEPS[b], STEPS[b + 1])
        both = jnp.dot(rows, s_ref[:, cols], preferred_element_type=jnp.float32)
        qt = (both[0:RANK] + both[RANK : 2 * RANK]) * (1.0 / REPLICAS)
        qt_v[:, cols] = qt
        high, low = halves(qt)
        product = jnp.dot(
            thrice, jnp.concatenate([high, low, high], axis=0), preferred_element_type=jnp.float32
        )
        new_v[:, cols] = (c_ref[:, cols] - product).astype(jnp.bfloat16)
        copies.append(pltpu.make_async_copy(new_v.at[:, cols], new_hbm.at[0, :, cols], store_sem.at[b + 2]))
        copies[-1].start()
    copies.append(pltpu.make_async_copy(qt_v, qt_hbm, store_sem.at[1]))
    copies[-1].start()
    for copy in copies:
        copy.wait()


def factor_call(tiles, split, corrected):
    hbm = pl.BlockSpec(memory_space=pltpu.HBM)
    vmem = pl.BlockSpec(memory_space=pltpu.VMEM)
    return pl.pallas_call(
        factor_kernel,
        out_shape=(
            jax.ShapeDtypeStruct((4, RANK), jnp.float32),
            jax.ShapeDtypeStruct((RANK, COLS), jnp.float32),
            jax.ShapeDtypeStruct((1, ROWS, COLS), jnp.bfloat16),
        ),
        in_specs=[vmem, vmem, vmem],
        out_specs=(hbm, hbm, hbm),
        scratch_shapes=[
            pltpu.VMEM((ROWS + 8, RANK), jnp.float32),
            pltpu.VMEM((RANK, COLS), jnp.float32),
            pltpu.VMEM((ROWS, COLS), jnp.bfloat16),
            pltpu.SemaphoreType.DMA((len(STEPS) + 1,)),
        ],
        compiler_params=pltpu.CompilerParams(vmem_limit_bytes=32 << 20),
        name="factors",
    )(tiles, split, corrected)


def local(gradients, error_memory, q_start):
    tiles, split, corrected = reduce_call(gradients, error_memory, q_start.T)
    p_rows, qt, new_error = factor_call(tiles, split, corrected)
    return p_rows, qt.T, new_error


def solution(mesh):
    in_specs = (P("dp", None, "tensor"), P("dp", None, "tensor"), P("tensor", None))
    out_specs = (P("tensor", None), P("tensor", None), P("dp", None, "tensor"))
    return jax.shard_map(local, mesh=mesh, in_specs=in_specs, out_specs=out_specs, check_vma=False)
```

```python
import jax
import jax.numpy as jnp
from jax import lax
from jax.experimental import pallas as pl
from jax.experimental.pallas import tpu as pltpu
from jax.sharding import PartitionSpec as P

MESH = pl.DeviceIdType.MESH
SIDE = 4
OFFSETS = sorted(
    ((dx, dy) for dx in range(SIDE) for dy in range(SIDE) if dx or dy),
    key=lambda d: -(min(d[0], SIDE - d[0]) + min(d[1], SIDE - d[1])),
)
HIGH = lax.Precision.HIGHEST
ROWS = 128
COLS = 896
HALF = 448
RANK = 32
CHIPS = 16
OWNERS = 14
SLICE = 32
SOURCES = 2 * OWNERS
DEPTH = 32
PLANE = 32
P_TILES = 4
P_STRIDE = 5
REPLICAS = 32
BLOCK = 16
STEPS = (0, 256, 512, 896)
VMEM_LIMIT = (64 << 20) - (1120 << 10)


def dot(left, right, left_dim, right_dim):
    return lax.dot_general(
        left,
        right,
        (((left_dim,), (right_dim,)), ((), ())),
        precision=HIGH,
        preferred_element_type=jnp.float32,
    )


def halves(value):
    high = value.astype(jnp.bfloat16)
    return high, (value - high.astype(jnp.float32)).astype(jnp.bfloat16)


def gram_of(value):
    high = value.astype(jnp.bfloat16)
    rest = value - high.astype(jnp.float32)
    middle = rest.astype(jnp.bfloat16)
    low = (rest - middle.astype(jnp.float32)).astype(jnp.bfloat16)
    left = jnp.concatenate([high, high, high, middle, middle, low], axis=0)
    right = jnp.concatenate([high, middle, low, high, middle, high], axis=0)
    return lax.dot_general(left, right, (((0,), (0,)), ((), ())), preferred_element_type=jnp.float32)


def wait_bytes(ref, sem):
    pltpu.make_async_copy(ref, ref, sem).wait()


def shifted(chip, offset):
    x, y = lax.div(chip, SIDE), lax.rem(chip, SIDE)
    return SIDE * lax.rem(x + offset[0], SIDE) + lax.rem(y + offset[1], SIDE)


def reduce_kernel(
    g_hbm, e_hbm, qt_hbm, m_out, s_out, c_out, first_out,
    g_v, e_v, qt_v, ct, sib, rs, part, tiles, zb, st_v, p_part, p_tiles, p_zb, p_v,
    load_sem, swap_sem, rs_sem, tile_sem, z_sem, m_sem, st_sem, pt_sem, pz_sem, p_sem, go_sem, later_sem,
):
    dp = lax.axis_index("dp")
    z = lax.axis_index("tensor")
    core = lax.rem(dp, 2)
    chip = lax.div(dp, 2)
    holds_p = jnp.logical_and(core == 1, lax.rem(chip, P_STRIDE) == 0)
    p_mine = lax.div(chip, P_STRIDE)

    def send(src, dst, sems, device):
        pltpu.make_async_remote_copy(
            src_ref=src, dst_ref=dst, send_sem=sems.at[0], recv_sem=sems.at[1],
            device_id=device, device_id_type=MESH,
        ).start()

    def send_line(buffer, sems):
        @pl.loop(0, DEPTH - 1)
        def _(k):
            half = lax.div(k + 1, 2)
            shift = jnp.where(lax.rem(k, 2) == 0, DEPTH // 2 + half, DEPTH // 2 - half)
            send(buffer.at[z], buffer.at[z], sems, (dp, lax.rem(z + shift, DEPTH)))

    def send_plane(ref, sems):
        for offset in OFFSETS:
            j = shifted(chip, offset)
            send(ref, ref, sems, (2 * j, z))
            send(ref, ref, sems, (2 * j + 1, z))
        send(ref, ref, sems, (dp - 1, z))

    loads = [
        pltpu.make_async_copy(g_hbm.at[0], g_v, load_sem.at[0]),
        pltpu.make_async_copy(e_hbm.at[0], e_v, load_sem.at[1]),
        pltpu.make_async_copy(qt_hbm, qt_v, load_sem.at[2]),
    ]
    for load in loads:
        load.start()

    barrier = pltpu.get_barrier_semaphore()

    for offset in OFFSETS:
        pl.semaphore_signal(barrier, inc=1, device_id=(2 * shifted(chip, offset), z), device_id_type=MESH)

    @pl.when(core == 1)
    def _():
        pl.semaphore_signal(barrier, inc=1, device_id=(dp - 1, z), device_id_type=MESH)

        @pl.loop(1, DEPTH)
        def _(k):
            pl.semaphore_signal(
                barrier, inc=1, device_id=(dp, lax.rem(z + k, DEPTH)), device_id_type=MESH
            )

    for load in loads:
        load.wait()
    for b in range(COLS // 128):
        cols = slice(128 * b, 128 * b + 128)
        corrected = g_v[:, cols] + e_v[:, cols].astype(jnp.float32)
        c_out[:, cols] = corrected
        ct[cols, :] = corrected.T

    def left_terms():
        p_part[...] = dot(qt_v[...], ct[...], 1, 0).reshape(P_TILES, 8, ROWS)

    @pl.when(core == 0)
    def _():
        pl.semaphore_wait(barrier, PLANE - 1)
        pl.semaphore_signal(go_sem, inc=1, device_id=(dp + 1, z), device_id_type=MESH)

    @pl.when(core == 1)
    def _():
        left_terms()
        pl.semaphore_wait(go_sem, 1)

    mine = core * HALF
    other = (1 - core) * HALF
    sibling = dp + 1 - 2 * core

    swap = pltpu.make_async_remote_copy(
        src_ref=ct.at[pl.ds(pl.multiple_of(other, 8), HALF)], dst_ref=sib,
        send_sem=swap_sem.at[0], recv_sem=swap_sem.at[1], device_id=(sibling, z), device_id_type=MESH,
    )
    swap.start()

    @pl.when(core == 0)
    def _():
        left_terms()

    for t in range(P_TILES):
        target = 2 * P_STRIDE * t + 1

        @pl.when(dp != target)
        def _():
            send(p_part.at[t], p_tiles.at[dp], pt_sem, (target, z))

    swap.wait_recv()
    ct[pl.ds(pl.multiple_of(mine, 8), HALF), :] += sib[...]
    for offset in OFFSETS:
        j = shifted(chip, offset)

        @pl.when(j < OWNERS)
        def _():
            piece = pl.ds(pl.multiple_of(mine + SLICE * j, 8), SLICE)
            send(ct.at[piece], rs.at[chip], rs_sem, (2 * j + core, z))

    slot = lax.min(chip, OWNERS - 1)
    own = pl.ds(pl.multiple_of(mine + SLICE * slot, 8), SLICE)
    source = core * OWNERS + slot

    @pl.when(chip < OWNERS)
    def _():
        rs[chip] = ct[own, :]
        wait_bytes(rs.at[pl.ds(0, CHIPS - 1)], rs_sem.at[1])
        total = rs[0]
        for j in range(1, CHIPS):
            total += rs[j]
        part[...] = gram_of(total).reshape(CHIPS, 8, ROWS)
        st_v[own, :] = total

        for offset in OFFSETS:
            j = shifted(chip, offset)
            send(part.at[j], tiles.at[source], tile_sem, (2 * j + 1, z))

        @pl.when(core == 0)
        def _():
            send(part.at[chip], tiles.at[source], tile_sem, (dp + 1, z))

    @pl.when(core == 1)
    def _():
        pl.semaphore_wait(barrier, DEPTH - 1)

        @pl.when(holds_p)
        def _():
            p_tiles[dp] = p_part[p_mine]
            wait_bytes(p_tiles.at[pl.ds(0, PLANE - 1)], pt_sem.at[1])
            total = p_tiles[0]
            for j in range(1, PLANE):
                total += p_tiles[j]
            p_zb[z] = total
            send_line(p_zb, pz_sem)

        @pl.when(chip < OWNERS)
        def _():
            tiles[source] = part[chip]
            wait_bytes(tiles.at[pl.ds(0, SOURCES - 1)], tile_sem.at[1])

        @pl.when(chip >= OWNERS)
        def _():
            wait_bytes(tiles, tile_sem.at[1])

        total = tiles[0]
        for j in range(1, SOURCES):
            total += tiles[j]
        zb[z] = total
        send_line(zb, z_sem)
        pl.semaphore_signal(later_sem, inc=1, device_id=(dp - 1, z), device_id_type=MESH)

    @pl.when(core == 0)
    def _():
        pl.semaphore_wait(later_sem, 1)

    @pl.when(chip < OWNERS)
    def _():
        @pl.loop(1, PLANE)
        def _(k):
            send(st_v.at[own], st_v.at[own], st_sem, (lax.rem(dp + k, PLANE), z))

        wait_bytes(st_v.at[pl.ds(0, COLS - SLICE)], st_sem.at[1])

    @pl.when(chip >= OWNERS)
    def _():
        wait_bytes(st_v, st_sem.at[1])

    for b in range(COLS // 128):
        cols = slice(128 * b, 128 * b + 128)
        high, low = halves(st_v[cols, :].T)
        s_out[0:ROWS, cols] = high
        s_out[ROWS : 2 * ROWS, cols] = low

    @pl.when(holds_p)
    def _():
        wait_bytes(p_zb.at[pl.ds(0, DEPTH - 1)], pz_sem.at[1])
        total = p_zb[0]
        for j in range(1, DEPTH):
            total += p_zb[j]
        p_v[p_mine] = total
        send_plane(p_v.at[p_mine], p_sem)

    @pl.when(core == 1)
    def _():
        wait_bytes(zb.at[pl.ds(0, DEPTH - 1)], z_sem.at[1])
        total = zb[0]
        for j in range(1, DEPTH):
            total += zb[j]
        m_out[chip] = total
        send_plane(m_out.at[chip], m_sem)

    @pl.when(holds_p)
    def _():
        wait_bytes(p_v.at[pl.ds(0, P_TILES - 1)], p_sem.at[1])

    @pl.when(jnp.logical_not(holds_p))
    def _():
        wait_bytes(p_v, p_sem.at[1])

    first_out[...] = orthonormal_rows(p_v[...].reshape(RANK, ROWS))

    @pl.when(core == 0)
    def _():
        wait_bytes(m_out, m_sem.at[1])

    @pl.when(core == 1)
    def _():
        wait_bytes(m_out.at[pl.ds(0, CHIPS - 1)], m_sem.at[1])
        wait_bytes(zb.at[pl.ds(0, DEPTH - 1)], z_sem.at[0])
        wait_bytes(zb.at[pl.ds(0, PLANE - 1)], m_sem.at[0])

    swap.wait_send()

    @pl.when(holds_p)
    def _():
        wait_bytes(p_zb.at[pl.ds(0, DEPTH - 1)], pz_sem.at[0])
        wait_bytes(p_zb.at[pl.ds(0, PLANE - 1)], p_sem.at[0])
        wait_bytes(p_part.at[pl.ds(0, P_TILES - 1)], pt_sem.at[0])

    @pl.when(jnp.logical_not(holds_p))
    def _():
        wait_bytes(p_part, pt_sem.at[0])

    @pl.when(chip < OWNERS)
    def _():
        wait_bytes(ct.at[pl.ds(0, SLICE * (OWNERS - 1))], rs_sem.at[0])
        wait_bytes(st_v, st_sem.at[0])
        wait_bytes(st_v.at[pl.ds(0, COLS // 28 * 3)], st_sem.at[0])

        @pl.when(core == 0)
        def _():
            wait_bytes(part, tile_sem.at[0])

        @pl.when(core == 1)
        def _():
            wait_bytes(part.at[pl.ds(0, CHIPS - 1)], tile_sem.at[0])

    @pl.when(chip >= OWNERS)
    def _():
        wait_bytes(ct.at[pl.ds(0, HALF)], rs_sem.at[0])


def reduce_call(gradients, error_memory, qt_start):
    hbm = pl.BlockSpec(memory_space=pltpu.HBM)
    vmem = pl.BlockSpec(memory_space=pltpu.VMEM)
    pair = pltpu.SemaphoreType.DMA((2,))
    return pl.pallas_call(
        reduce_kernel,
        out_shape=(
            pltpu.VMEM((CHIPS, 8, ROWS), jnp.float32),
            pltpu.VMEM((2 * ROWS, COLS), jnp.bfloat16),
            pltpu.VMEM((ROWS, COLS), jnp.float32),
            pltpu.VMEM((RANK, ROWS), jnp.float32),
        ),
        in_specs=[hbm] * 3,
        out_specs=(vmem,) * 4,
        scratch_shapes=[
            pltpu.VMEM((ROWS, COLS), jnp.float32),
            pltpu.VMEM((ROWS, COLS), jnp.bfloat16),
            pltpu.VMEM((RANK, COLS), jnp.float32),
            pltpu.VMEM((COLS, ROWS), jnp.float32),
            pltpu.VMEM((HALF, ROWS), jnp.float32),
            pltpu.VMEM((CHIPS, SLICE, ROWS), jnp.float32),
            pltpu.VMEM((CHIPS, 8, ROWS), jnp.float32),
            pltpu.VMEM((SOURCES, 8, ROWS), jnp.float32),
            pltpu.VMEM((DEPTH, 8, ROWS), jnp.float32),
            pltpu.VMEM((COLS, ROWS), jnp.float32),
            pltpu.VMEM((P_TILES, 8, ROWS), jnp.float32),
            pltpu.VMEM((PLANE, 8, ROWS), jnp.float32),
            pltpu.VMEM((DEPTH, 8, ROWS), jnp.float32),
            pltpu.VMEM((P_TILES, 8, ROWS), jnp.float32),
            pltpu.SemaphoreType.DMA((3,)),
            pair, pair, pair, pair, pair, pair, pair, pair, pair,
            pltpu.SemaphoreType.REGULAR,
            pltpu.SemaphoreType.REGULAR,
        ],
        compiler_params=pltpu.CompilerParams(
            collective_id=0, has_side_effects=True, vmem_limit_bytes=VMEM_LIMIT
        ),
        name="plane_and_line_sums",
    )(gradients, error_memory, qt_start)


def orthonormal_rows(pt):
    gram = dot(pt, pt, 1, 1)
    high = RANK // 8
    gram = [gram[8 * t : 8 * t + 8] for t in range(high)]
    rows = [pt[8 * t : 8 * t + 8] for t in range(high)]
    pivots = [jnp.ones((8, ROWS), jnp.float32) for t in range(high)]
    sub = lax.broadcasted_iota(jnp.int32, (8, ROWS), 0)
    for first in range(0, RANK, BLOCK):
        more = first + BLOCK < RANK
        cols = [
            [jnp.broadcast_to(gram[t][:, first + j : first + j + 1], (8, ROWS)) for t in range(high)]
            for j in range(BLOCK)
        ]
        for j in range(BLOCK):
            at, s = divmod(first + j, 8)
            pivot = jnp.broadcast_to(cols[j][at][s : s + 1], (8, ROWS))
            inverse = 1.0 / pivot
            factor = [None] * high
            for t in range(at, high):
                factor[t] = cols[j][t] * inverse
            factor[at] = jnp.where(sub > s, factor[at], 0.0)
            for later in range(j + 1, BLOCK):
                entry = jnp.broadcast_to(cols[later][at][s : s + 1], (8, ROWS))
                for t in range(at, high):
                    cols[later][t] = cols[later][t] - factor[t] * entry
            row = jnp.broadcast_to(rows[at][s : s + 1], (8, ROWS))
            for t in range(at, high):
                rows[t] = rows[t] - factor[t] * row
            if more:
                line = jnp.broadcast_to(gram[at][s : s + 1], (8, RANK))
                for t in range(at, high):
                    gram[t] = gram[t] - factor[t][:, :RANK] * line
            pivots[at] = jnp.where(sub == s, pivot, pivots[at])
    return jnp.concatenate([rows[t] / jnp.sqrt(pivots[t]) for t in range(high)], axis=0)


def factor_kernel(m_ref, s_ref, c_ref, first_ref, p_hbm, qt_hbm, new_hbm, p_v, qt_v, new_v, store_sem):
    second = dot(first_ref[...], m_ref[...].reshape(ROWS, ROWS), 1, 0) * (1.0 / REPLICAS)
    pt = orthonormal_rows(second)
    left = pt.T
    z = lax.axis_index("tensor")
    p_v[0:ROWS, :] = left
    pair = p_v[pl.ds(pl.multiple_of(8 * lax.div(z, 2), 8), 8), :]
    p_v[ROWS : ROWS + 4, :] = jnp.where(lax.rem(z, 2) == 0, pair[0:4], pair[4:8])
    copies = [pltpu.make_async_copy(p_v.at[pl.ds(ROWS, 4)], p_hbm, store_sem.at[0])]
    copies[0].start()

    high, low = halves(pt)
    zero = jnp.zeros_like(low)
    rows = jnp.concatenate(
        [jnp.concatenate([high, high], axis=1), jnp.concatenate([low, zero], axis=1)], axis=0
    )
    high, low = halves(left)
    thrice = jnp.concatenate([high, high, low], axis=1)
    for b in range(len(STEPS) - 1):
        cols = slice(STEPS[b], STEPS[b + 1])
        both = jnp.dot(rows, s_ref[:, cols], preferred_element_type=jnp.float32)
        qt = (both[0:RANK] + both[RANK : 2 * RANK]) * (1.0 / REPLICAS)
        qt_v[:, cols] = qt
        high, low = halves(qt)
        product = jnp.dot(
            thrice, jnp.concatenate([high, low, high], axis=0), preferred_element_type=jnp.float32
        )
        new_v[:, cols] = (c_ref[:, cols] - product).astype(jnp.bfloat16)
        copies.append(pltpu.make_async_copy(new_v.at[:, cols], new_hbm.at[0, :, cols], store_sem.at[b + 2]))
        copies[-1].start()
    copies.append(pltpu.make_async_copy(qt_v, qt_hbm, store_sem.at[1]))
    copies[-1].start()
    for copy in copies:
        copy.wait()


def factor_call(tiles, split, corrected, first):
    hbm = pl.BlockSpec(memory_space=pltpu.HBM)
    vmem = pl.BlockSpec(memory_space=pltpu.VMEM)
    return pl.pallas_call(
        factor_kernel,
        out_shape=(
            jax.ShapeDtypeStruct((4, RANK), jnp.float32),
            jax.ShapeDtypeStruct((RANK, COLS), jnp.float32),
            jax.ShapeDtypeStruct((1, ROWS, COLS), jnp.bfloat16),
        ),
        in_specs=[vmem, vmem, vmem, vmem],
        out_specs=(hbm, hbm, hbm),
        scratch_shapes=[
            pltpu.VMEM((ROWS + 8, RANK), jnp.float32),
            pltpu.VMEM((RANK, COLS), jnp.float32),
            pltpu.VMEM((ROWS, COLS), jnp.bfloat16),
            pltpu.SemaphoreType.DMA((len(STEPS) + 1,)),
        ],
        compiler_params=pltpu.CompilerParams(vmem_limit_bytes=32 << 20),
        name="factors",
    )(tiles, split, corrected, first)


def local(gradients, error_memory, q_start):
    tiles, split, corrected, first = reduce_call(gradients, error_memory, q_start.T)
    p_rows, qt, new_error = factor_call(tiles, split, corrected, first)
    return p_rows, qt.T, new_error


def solution(mesh):
    in_specs = (P("dp", None, "tensor"), P("dp", None, "tensor"), P("tensor", None))
    out_specs = (P("tensor", None), P("tensor", None), P("dp", None, "tensor"))
    return jax.shard_map(local, mesh=mesh, in_specs=in_specs, out_specs=out_specs, check_vma=False)
```

```python
import jax
import jax.numpy as jnp
from jax import lax
from jax.experimental import pallas as pl
from jax.experimental.pallas import tpu as pltpu
from jax.sharding import PartitionSpec as P

MESH = pl.DeviceIdType.MESH
SIDE = 4
OFFSETS = sorted(
    ((dx, dy) for dx in range(SIDE) for dy in range(SIDE) if dx or dy),
    key=lambda d: -(min(d[0], SIDE - d[0]) + min(d[1], SIDE - d[1])),
)
HIGH = lax.Precision.HIGHEST
ROWS = 128
COLS = 896
HALF = 448
RANK = 32
CHIPS = 16
OWNERS = 14
SLICE = 32
SOURCES = 2 * OWNERS
DEPTH = 32
PLANE = 32
P_TILES = 4
P_STRIDE = 5
REPLICAS = 32
BLOCK = 16
STEPS = (0, 896)
VMEM_LIMIT = (64 << 20) - (1120 << 10)


def dot(left, right, left_dim, right_dim):
    return lax.dot_general(
        left,
        right,
        (((left_dim,), (right_dim,)), ((), ())),
        precision=HIGH,
        preferred_element_type=jnp.float32,
    )


def halves(value):
    high = value.astype(jnp.bfloat16)
    return high, (value - high.astype(jnp.float32)).astype(jnp.bfloat16)


def gram_of(value):
    high = value.astype(jnp.bfloat16)
    rest = value - high.astype(jnp.float32)
    middle = rest.astype(jnp.bfloat16)
    low = (rest - middle.astype(jnp.float32)).astype(jnp.bfloat16)
    left = jnp.concatenate([high, high, high, middle, middle, low], axis=0)
    right = jnp.concatenate([high, middle, low, high, middle, high], axis=0)
    return lax.dot_general(left, right, (((0,), (0,)), ((), ())), preferred_element_type=jnp.float32)


def wait_bytes(ref, sem):
    pltpu.make_async_copy(ref, ref, sem).wait()


def shifted(chip, offset):
    x, y = lax.div(chip, SIDE), lax.rem(chip, SIDE)
    return SIDE * lax.rem(x + offset[0], SIDE) + lax.rem(y + offset[1], SIDE)


def reduce_kernel(
    g_hbm, e_hbm, qt_hbm, m_out, s_out, c_out, first_out,
    g_v, e_v, qt_v, ct, sib, rs, part, tiles, zb, st_v, p_part, p_tiles, p_zb, p_v,
    load_sem, swap_sem, rs_sem, tile_sem, z_sem, m_sem, st_sem, pt_sem, pz_sem, p_sem, go_sem, later_sem,
):
    dp = lax.axis_index("dp")
    z = lax.axis_index("tensor")
    core = lax.rem(dp, 2)
    chip = lax.div(dp, 2)
    holds_p = jnp.logical_and(core == 1, lax.rem(chip, P_STRIDE) == 0)
    p_mine = lax.div(chip, P_STRIDE)

    def send(src, dst, sems, device):
        pltpu.make_async_remote_copy(
            src_ref=src, dst_ref=dst, send_sem=sems.at[0], recv_sem=sems.at[1],
            device_id=device, device_id_type=MESH,
        ).start()

    def send_line(buffer, sems):
        @pl.loop(0, DEPTH - 1)
        def _(k):
            half = lax.div(k + 1, 2)
            shift = jnp.where(lax.rem(k, 2) == 0, DEPTH // 2 + half, DEPTH // 2 - half)
            send(buffer.at[z], buffer.at[z], sems, (dp, lax.rem(z + shift, DEPTH)))

    def send_plane(ref, sems):
        for offset in OFFSETS:
            j = shifted(chip, offset)
            send(ref, ref, sems, (2 * j, z))
            send(ref, ref, sems, (2 * j + 1, z))
        send(ref, ref, sems, (dp - 1, z))

    loads = [
        pltpu.make_async_copy(g_hbm.at[0], g_v, load_sem.at[0]),
        pltpu.make_async_copy(e_hbm.at[0], e_v, load_sem.at[1]),
        pltpu.make_async_copy(qt_hbm, qt_v, load_sem.at[2]),
    ]
    for load in loads:
        load.start()

    barrier = pltpu.get_barrier_semaphore()

    for offset in OFFSETS:
        pl.semaphore_signal(barrier, inc=1, device_id=(2 * shifted(chip, offset), z), device_id_type=MESH)

    @pl.when(core == 1)
    def _():
        pl.semaphore_signal(barrier, inc=1, device_id=(dp - 1, z), device_id_type=MESH)

        @pl.loop(1, DEPTH)
        def _(k):
            pl.semaphore_signal(
                barrier, inc=1, device_id=(dp, lax.rem(z + k, DEPTH)), device_id_type=MESH
            )

    for load in loads:
        load.wait()
    for b in range(COLS // 128):
        cols = slice(128 * b, 128 * b + 128)
        corrected = g_v[:, cols] + e_v[:, cols].astype(jnp.float32)
        c_out[:, cols] = corrected
        ct[cols, :] = corrected.T
    p_part[...] = dot(qt_v[...], ct[...], 1, 0).reshape(P_TILES, 8, ROWS)

    @pl.when(core == 0)
    def _():
        pl.semaphore_wait(barrier, PLANE - 1)
        pl.semaphore_signal(go_sem, inc=1, device_id=(dp + 1, z), device_id_type=MESH)

    @pl.when(core == 1)
    def _():
        pl.semaphore_wait(go_sem, 1)

    for t in range(P_TILES):
        target = 2 * P_STRIDE * t + 1

        @pl.when(dp != target)
        def _():
            send(p_part.at[t], p_tiles.at[dp], pt_sem, (target, z))

    mine = core * HALF
    other = (1 - core) * HALF
    sibling = dp + 1 - 2 * core

    swap = pltpu.make_async_remote_copy(
        src_ref=ct.at[pl.ds(pl.multiple_of(other, 8), HALF)], dst_ref=sib,
        send_sem=swap_sem.at[0], recv_sem=swap_sem.at[1], device_id=(sibling, z), device_id_type=MESH,
    )
    swap.start()

    swap.wait_recv()
    ct[pl.ds(pl.multiple_of(mine, 8), HALF), :] += sib[...]
    for offset in OFFSETS:
        j = shifted(chip, offset)

        @pl.when(j < OWNERS)
        def _():
            piece = pl.ds(pl.multiple_of(mine + SLICE * j, 8), SLICE)
            send(ct.at[piece], rs.at[chip], rs_sem, (2 * j + core, z))

    slot = lax.min(chip, OWNERS - 1)
    own = pl.ds(pl.multiple_of(mine + SLICE * slot, 8), SLICE)
    source = core * OWNERS + slot

    @pl.when(chip < OWNERS)
    def _():
        rs[chip] = ct[own, :]
        wait_bytes(rs.at[pl.ds(0, CHIPS - 1)], rs_sem.at[1])
        total = rs[0]
        for j in range(1, CHIPS):
            total += rs[j]
        part[...] = gram_of(total).reshape(CHIPS, 8, ROWS)
        st_v[own, :] = total

        for offset in OFFSETS:
            j = shifted(chip, offset)
            send(part.at[j], tiles.at[source], tile_sem, (2 * j + 1, z))

        @pl.when(core == 0)
        def _():
            send(part.at[chip], tiles.at[source], tile_sem, (dp + 1, z))

    @pl.when(core == 1)
    def _():
        pl.semaphore_wait(barrier, DEPTH - 1)

        @pl.when(holds_p)
        def _():
            p_tiles[dp] = p_part[p_mine]
            wait_bytes(p_tiles.at[pl.ds(0, PLANE - 1)], pt_sem.at[1])
            total = p_tiles[0]
            for j in range(1, PLANE):
                total += p_tiles[j]
            p_zb[z] = total
            send_line(p_zb, pz_sem)

        @pl.when(chip < OWNERS)
        def _():
            tiles[source] = part[chip]
            wait_bytes(tiles.at[pl.ds(0, SOURCES - 1)], tile_sem.at[1])

        @pl.when(chip >= OWNERS)
        def _():
            wait_bytes(tiles, tile_sem.at[1])

        total = tiles[0]
        for j in range(1, SOURCES):
            total += tiles[j]
        zb[z] = total
        send_line(zb, z_sem)
        pl.semaphore_signal(later_sem, inc=1, device_id=(dp - 1, z), device_id_type=MESH)

    @pl.when(core == 0)
    def _():
        pl.semaphore_wait(later_sem, 1)

    @pl.when(chip < OWNERS)
    def _():
        @pl.loop(1, PLANE)
        def _(k):
            send(st_v.at[own], st_v.at[own], st_sem, (lax.rem(dp + k, PLANE), z))

        wait_bytes(st_v.at[pl.ds(0, COLS - SLICE)], st_sem.at[1])

    @pl.when(chip >= OWNERS)
    def _():
        wait_bytes(st_v, st_sem.at[1])

    for b in range(COLS // 128):
        cols = slice(128 * b, 128 * b + 128)
        high, low = halves(st_v[cols, :].T)
        s_out[0:ROWS, cols] = high
        s_out[ROWS : 2 * ROWS, cols] = low

    @pl.when(holds_p)
    def _():
        wait_bytes(p_zb.at[pl.ds(0, DEPTH - 1)], pz_sem.at[1])
        total = p_zb[0]
        for j in range(1, DEPTH):
            total += p_zb[j]
        p_v[p_mine] = total
        send_plane(p_v.at[p_mine], p_sem)

    @pl.when(core == 1)
    def _():
        wait_bytes(zb.at[pl.ds(0, DEPTH - 1)], z_sem.at[1])
        total = zb[0]
        for j in range(1, DEPTH):
            total += zb[j]
        m_out[chip] = total
        send_plane(m_out.at[chip], m_sem)

    @pl.when(holds_p)
    def _():
        wait_bytes(p_v.at[pl.ds(0, P_TILES - 1)], p_sem.at[1])

    @pl.when(jnp.logical_not(holds_p))
    def _():
        wait_bytes(p_v, p_sem.at[1])

    first_out[...] = orthonormal_rows(p_v[...].reshape(RANK, ROWS))

    swap.wait_send()

    @pl.when(holds_p)
    def _():
        wait_bytes(p_zb.at[pl.ds(0, DEPTH - 1)], pz_sem.at[0])
        wait_bytes(p_zb.at[pl.ds(0, PLANE - 1)], p_sem.at[0])
        wait_bytes(p_part.at[pl.ds(0, P_TILES - 1)], pt_sem.at[0])

    @pl.when(jnp.logical_not(holds_p))
    def _():
        wait_bytes(p_part, pt_sem.at[0])

    @pl.when(chip < OWNERS)
    def _():
        wait_bytes(ct.at[pl.ds(0, SLICE * (OWNERS - 1))], rs_sem.at[0])
        wait_bytes(st_v, st_sem.at[0])
        wait_bytes(st_v.at[pl.ds(0, COLS // 28 * 3)], st_sem.at[0])

        @pl.when(core == 0)
        def _():
            wait_bytes(part, tile_sem.at[0])

        @pl.when(core == 1)
        def _():
            wait_bytes(part.at[pl.ds(0, CHIPS - 1)], tile_sem.at[0])

    @pl.when(chip >= OWNERS)
    def _():
        wait_bytes(ct.at[pl.ds(0, HALF)], rs_sem.at[0])

    @pl.when(core == 1)
    def _():
        wait_bytes(zb.at[pl.ds(0, DEPTH - 1)], z_sem.at[0])
        wait_bytes(zb.at[pl.ds(0, PLANE - 1)], m_sem.at[0])

    @pl.when(core == 0)
    def _():
        wait_bytes(m_out, m_sem.at[1])

    @pl.when(core == 1)
    def _():
        wait_bytes(m_out.at[pl.ds(0, CHIPS - 1)], m_sem.at[1])


def reduce_call(gradients, error_memory, qt_start):
    hbm = pl.BlockSpec(memory_space=pltpu.HBM)
    vmem = pl.BlockSpec(memory_space=pltpu.VMEM)
    pair = pltpu.SemaphoreType.DMA((2,))
    return pl.pallas_call(
        reduce_kernel,
        out_shape=(
            pltpu.VMEM((CHIPS, 8, ROWS), jnp.float32),
            pltpu.VMEM((2 * ROWS, COLS), jnp.bfloat16),
            pltpu.VMEM((ROWS, COLS), jnp.float32),
            pltpu.VMEM((RANK, ROWS), jnp.float32),
        ),
        in_specs=[hbm] * 3,
        out_specs=(vmem,) * 4,
        scratch_shapes=[
            pltpu.VMEM((ROWS, COLS), jnp.float32),
            pltpu.VMEM((ROWS, COLS), jnp.bfloat16),
            pltpu.VMEM((RANK, COLS), jnp.float32),
            pltpu.VMEM((COLS, ROWS), jnp.float32),
            pltpu.VMEM((HALF, ROWS), jnp.float32),
            pltpu.VMEM((CHIPS, SLICE, ROWS), jnp.float32),
            pltpu.VMEM((CHIPS, 8, ROWS), jnp.float32),
            pltpu.VMEM((SOURCES, 8, ROWS), jnp.float32),
            pltpu.VMEM((DEPTH, 8, ROWS), jnp.float32),
            pltpu.VMEM((COLS, ROWS), jnp.float32),
            pltpu.VMEM((P_TILES, 8, ROWS), jnp.float32),
            pltpu.VMEM((PLANE, 8, ROWS), jnp.float32),
            pltpu.VMEM((DEPTH, 8, ROWS), jnp.float32),
            pltpu.VMEM((P_TILES, 8, ROWS), jnp.float32),
            pltpu.SemaphoreType.DMA((3,)),
            pair, pair, pair, pair, pair, pair, pair, pair, pair,
            pltpu.SemaphoreType.REGULAR,
            pltpu.SemaphoreType.REGULAR,
        ],
        compiler_params=pltpu.CompilerParams(
            collective_id=0, has_side_effects=True, vmem_limit_bytes=VMEM_LIMIT
        ),
        name="plane_and_line_sums",
    )(gradients, error_memory, qt_start)


def orthonormal_rows(pt):
    gram = dot(pt, pt, 1, 1)
    high = RANK // 8
    gram = [gram[8 * t : 8 * t + 8] for t in range(high)]
    rows = [pt[8 * t : 8 * t + 8] for t in range(high)]
    pivots = [jnp.ones((8, ROWS), jnp.float32) for t in range(high)]
    sub = lax.broadcasted_iota(jnp.int32, (8, ROWS), 0)
    for first in range(0, RANK, BLOCK):
        more = first + BLOCK < RANK
        cols = [
            [jnp.broadcast_to(gram[t][:, first + j : first + j + 1], (8, ROWS)) for t in range(high)]
            for j in range(BLOCK)
        ]
        for j in range(BLOCK):
            at, s = divmod(first + j, 8)
            pivot = jnp.broadcast_to(cols[j][at][s : s + 1], (8, ROWS))
            inverse = 1.0 / pivot
            factor = [None] * high
            for t in range(at, high):
                factor[t] = cols[j][t] * inverse
            factor[at] = jnp.where(sub > s, factor[at], 0.0)
            for later in range(j + 1, BLOCK):
                entry = jnp.broadcast_to(cols[later][at][s : s + 1], (8, ROWS))
                for t in range(at, high):
                    cols[later][t] = cols[later][t] - factor[t] * entry
            row = jnp.broadcast_to(rows[at][s : s + 1], (8, ROWS))
            for t in range(at, high):
                rows[t] = rows[t] - factor[t] * row
            if more:
                line = jnp.broadcast_to(gram[at][s : s + 1], (8, RANK))
                for t in range(at, high):
                    gram[t] = gram[t] - factor[t][:, :RANK] * line
            pivots[at] = jnp.where(sub == s, pivot, pivots[at])
    return jnp.concatenate([rows[t] / jnp.sqrt(pivots[t]) for t in range(high)], axis=0)


def factor_kernel(m_ref, s_ref, c_ref, first_ref, p_hbm, qt_hbm, new_hbm, p_v, qt_v, new_v, store_sem):
    second = dot(first_ref[...], m_ref[...].reshape(ROWS, ROWS), 1, 0) * (1.0 / REPLICAS)
    pt = orthonormal_rows(second)
    left = pt.T
    z = lax.axis_index("tensor")
    p_v[0:ROWS, :] = left
    pair = p_v[pl.ds(pl.multiple_of(8 * lax.div(z, 2), 8), 8), :]
    p_v[ROWS : ROWS + 4, :] = jnp.where(lax.rem(z, 2) == 0, pair[0:4], pair[4:8])
    copies = [pltpu.make_async_copy(p_v.at[pl.ds(ROWS, 4)], p_hbm, store_sem.at[0])]
    copies[0].start()

    high, low = halves(pt)
    zero = jnp.zeros_like(low)
    rows = jnp.concatenate(
        [jnp.concatenate([high, high], axis=1), jnp.concatenate([low, zero], axis=1)], axis=0
    )
    high, low = halves(left)
    thrice = jnp.concatenate([high, high, low], axis=1)
    for b in range(len(STEPS) - 1):
        cols = slice(STEPS[b], STEPS[b + 1])
        both = jnp.dot(rows, s_ref[:, cols], preferred_element_type=jnp.float32)
        qt = (both[0:RANK] + both[RANK : 2 * RANK]) * (1.0 / REPLICAS)
        qt_v[:, cols] = qt
        high, low = halves(qt)
        product = jnp.dot(
            thrice, jnp.concatenate([high, low, high], axis=0), preferred_element_type=jnp.float32
        )
        new_v[:, cols] = (c_ref[:, cols] - product).astype(jnp.bfloat16)
        copies.append(pltpu.make_async_copy(new_v.at[:, cols], new_hbm.at[0, :, cols], store_sem.at[b + 2]))
        copies[-1].start()
    copies.append(pltpu.make_async_copy(qt_v, qt_hbm, store_sem.at[1]))
    copies[-1].start()
    for copy in copies:
        copy.wait()


def factor_call(tiles, split, corrected, first):
    hbm = pl.BlockSpec(memory_space=pltpu.HBM)
    vmem = pl.BlockSpec(memory_space=pltpu.VMEM)
    return pl.pallas_call(
        factor_kernel,
        out_shape=(
            jax.ShapeDtypeStruct((4, RANK), jnp.float32),
            jax.ShapeDtypeStruct((RANK, COLS), jnp.float32),
            jax.ShapeDtypeStruct((1, ROWS, COLS), jnp.bfloat16),
        ),
        in_specs=[vmem, vmem, vmem, vmem],
        out_specs=(hbm, hbm, hbm),
        scratch_shapes=[
            pltpu.VMEM((ROWS + 8, RANK), jnp.float32),
            pltpu.VMEM((RANK, COLS), jnp.float32),
            pltpu.VMEM((ROWS, COLS), jnp.bfloat16),
            pltpu.SemaphoreType.DMA((len(STEPS) + 1,)),
        ],
        compiler_params=pltpu.CompilerParams(vmem_limit_bytes=32 << 20),
        name="factors",
    )(tiles, split, corrected, first)


def local(gradients, error_memory, q_start):
    tiles, split, corrected, first = reduce_call(gradients, error_memory, q_start.T)
    p_rows, qt, new_error = factor_call(tiles, split, corrected, first)
    return p_rows, qt.T, new_error


def solution(mesh):
    in_specs = (P("dp", None, "tensor"), P("dp", None, "tensor"), P("tensor", None))
    out_specs = (P("tensor", None), P("tensor", None), P("dp", None, "tensor"))
    return jax.shard_map(local, mesh=mesh, in_specs=in_specs, out_specs=out_specs, check_vma=False)
```

```python
import jax
import jax.numpy as jnp
from jax import lax
from jax.experimental import pallas as pl
from jax.experimental.pallas import tpu as pltpu
from jax.sharding import PartitionSpec as P

MESH = pl.DeviceIdType.MESH
SIDE = 4
OFFSETS = sorted(
    ((dx, dy) for dx in range(SIDE) for dy in range(SIDE) if dx or dy),
    key=lambda d: -(min(d[0], SIDE - d[0]) + min(d[1], SIDE - d[1])),
)
HIGH = lax.Precision.HIGHEST
ROWS = 128
COLS = 896
HALF = 448
RANK = 32
CHIPS = 16
OWNERS = 14
SLICE = 32
SOURCES = 2 * OWNERS
DEPTH = 32
PLANE = 32
P_TILES = 4
P_STRIDE = 5
REPLICAS = 32
BLOCK = 16
STEPS = (0, 896)
VMEM_LIMIT = (64 << 20) - (1120 << 10)


def dot(left, right, left_dim, right_dim):
    return lax.dot_general(
        left,
        right,
        (((left_dim,), (right_dim,)), ((), ())),
        precision=HIGH,
        preferred_element_type=jnp.float32,
    )


def halves(value):
    high = value.astype(jnp.bfloat16)
    return high, (value - high.astype(jnp.float32)).astype(jnp.bfloat16)


def gram_of(value):
    high = value.astype(jnp.bfloat16)
    rest = value - high.astype(jnp.float32)
    middle = rest.astype(jnp.bfloat16)
    low = (rest - middle.astype(jnp.float32)).astype(jnp.bfloat16)
    left = jnp.concatenate([high, high, high, middle, middle, low], axis=0)
    right = jnp.concatenate([high, middle, low, high, middle, high], axis=0)
    return lax.dot_general(left, right, (((0,), (0,)), ((), ())), preferred_element_type=jnp.float32)


def wait_bytes(ref, sem):
    pltpu.make_async_copy(ref, ref, sem).wait()


def shifted(chip, offset):
    x, y = lax.div(chip, SIDE), lax.rem(chip, SIDE)
    return SIDE * lax.rem(x + offset[0], SIDE) + lax.rem(y + offset[1], SIDE)


def reduce_kernel(
    g_hbm, e_hbm, qt_hbm, m_out, s_out, c_out, first_out,
    g_v, e_v, qt_v, ct, sib, rs, part, tiles, zb, st_v, p_part, p_tiles, p_zb, p_v,
    load_sem, swap_sem, rs_sem, tile_sem, z_sem, m_sem, st_sem, pt_sem, pz_sem, p_sem, go_sem, later_sem,
):
    dp = lax.axis_index("dp")
    z = lax.axis_index("tensor")
    core = lax.rem(dp, 2)
    chip = lax.div(dp, 2)
    holds_p = jnp.logical_and(core == 1, lax.rem(chip, P_STRIDE) == 0)
    p_mine = lax.div(chip, P_STRIDE)

    def send(src, dst, sems, device):
        pltpu.make_async_remote_copy(
            src_ref=src, dst_ref=dst, send_sem=sems.at[0], recv_sem=sems.at[1],
            device_id=device, device_id_type=MESH,
        ).start()

    def send_line(buffer, sems):
        @pl.loop(0, DEPTH - 1)
        def _(k):
            half = lax.div(k + 1, 2)
            shift = jnp.where(lax.rem(k, 2) == 0, DEPTH // 2 + half, DEPTH // 2 - half)
            send(buffer.at[z], buffer.at[z], sems, (dp, lax.rem(z + shift, DEPTH)))

    def send_plane(ref, sems):
        for offset in OFFSETS:
            j = shifted(chip, offset)
            send(ref, ref, sems, (2 * j, z))
            send(ref, ref, sems, (2 * j + 1, z))
        send(ref, ref, sems, (dp - 1, z))

    loads = [
        pltpu.make_async_copy(g_hbm.at[0], g_v, load_sem.at[0]),
        pltpu.make_async_copy(e_hbm.at[0], e_v, load_sem.at[1]),
        pltpu.make_async_copy(qt_hbm, qt_v, load_sem.at[2]),
    ]
    for load in loads:
        load.start()

    barrier = pltpu.get_barrier_semaphore()

    for offset in OFFSETS:
        pl.semaphore_signal(barrier, inc=1, device_id=(2 * shifted(chip, offset), z), device_id_type=MESH)

    @pl.when(core == 1)
    def _():
        pl.semaphore_signal(barrier, inc=1, device_id=(dp - 1, z), device_id_type=MESH)

        @pl.loop(1, DEPTH)
        def _(k):
            pl.semaphore_signal(
                barrier, inc=1, device_id=(dp, lax.rem(z + k, DEPTH)), device_id_type=MESH
            )

    for load in loads:
        load.wait()
    for b in range(COLS // 128):
        cols = slice(128 * b, 128 * b + 128)
        corrected = g_v[:, cols] + e_v[:, cols].astype(jnp.float32)
        c_out[:, cols] = corrected
        ct[cols, :] = corrected.T

    def left_terms():
        p_part[...] = dot(qt_v[...], ct[...], 1, 0).reshape(P_TILES, 8, ROWS)

    @pl.when(core == 0)
    def _():
        pl.semaphore_wait(barrier, PLANE - 1)
        pl.semaphore_signal(go_sem, inc=1, device_id=(dp + 1, z), device_id_type=MESH)

    @pl.when(core == 1)
    def _():
        left_terms()
        pl.semaphore_wait(go_sem, 1)

    mine = core * HALF
    other = (1 - core) * HALF
    sibling = dp + 1 - 2 * core

    swap = pltpu.make_async_remote_copy(
        src_ref=ct.at[pl.ds(pl.multiple_of(other, 8), HALF)], dst_ref=sib,
        send_sem=swap_sem.at[0], recv_sem=swap_sem.at[1], device_id=(sibling, z), device_id_type=MESH,
    )
    swap.start()

    @pl.when(core == 0)
    def _():
        left_terms()

    for t in range(P_TILES):
        target = 2 * P_STRIDE * t + 1

        @pl.when(dp != target)
        def _():
            send(p_part.at[t], p_tiles.at[dp], pt_sem, (target, z))

    swap.wait_recv()
    ct[pl.ds(pl.multiple_of(mine, 8), HALF), :] += sib[...]
    for offset in OFFSETS:
        j = shifted(chip, offset)

        @pl.when(j < OWNERS)
        def _():
            piece = pl.ds(pl.multiple_of(mine + SLICE * j, 8), SLICE)
            send(ct.at[piece], rs.at[chip], rs_sem, (2 * j + core, z))

    slot = lax.min(chip, OWNERS - 1)
    own = pl.ds(pl.multiple_of(mine + SLICE * slot, 8), SLICE)
    source = core * OWNERS + slot

    @pl.when(chip < OWNERS)
    def _():
        rs[chip] = ct[own, :]
        wait_bytes(rs.at[pl.ds(0, CHIPS - 1)], rs_sem.at[1])
        total = rs[0]
        for j in range(1, CHIPS):
            total += rs[j]
        part[...] = gram_of(total).reshape(CHIPS, 8, ROWS)
        st_v[own, :] = total

        for offset in OFFSETS:
            j = shifted(chip, offset)
            send(part.at[j], tiles.at[source], tile_sem, (2 * j + 1, z))

        @pl.when(core == 0)
        def _():
            send(part.at[chip], tiles.at[source], tile_sem, (dp + 1, z))

    @pl.when(core == 1)
    def _():
        pl.semaphore_wait(barrier, DEPTH - 1)

        @pl.when(holds_p)
        def _():
            p_tiles[dp] = p_part[p_mine]
            wait_bytes(p_tiles.at[pl.ds(0, PLANE - 1)], pt_sem.at[1])
            total = p_tiles[0]
            for j in range(1, PLANE):
                total += p_tiles[j]
            p_zb[z] = total
            send_line(p_zb, pz_sem)

        @pl.when(chip < OWNERS)
        def _():
            tiles[source] = part[chip]
            wait_bytes(tiles.at[pl.ds(0, SOURCES - 1)], tile_sem.at[1])

        @pl.when(chip >= OWNERS)
        def _():
            wait_bytes(tiles, tile_sem.at[1])

        total = tiles[0]
        for j in range(1, SOURCES):
            total += tiles[j]
        zb[z] = total
        send_line(zb, z_sem)
        pl.semaphore_signal(later_sem, inc=1, device_id=(dp - 1, z), device_id_type=MESH)

    @pl.when(core == 0)
    def _():
        pl.semaphore_wait(later_sem, 1)

    @pl.when(chip < OWNERS)
    def _():
        @pl.loop(1, PLANE)
        def _(k):
            send(st_v.at[own], st_v.at[own], st_sem, (lax.rem(dp + k, PLANE), z))

        wait_bytes(st_v.at[pl.ds(0, COLS - SLICE)], st_sem.at[1])

    @pl.when(chip >= OWNERS)
    def _():
        wait_bytes(st_v, st_sem.at[1])

    for b in range(COLS // 128):
        cols = slice(128 * b, 128 * b + 128)
        high, low = halves(st_v[cols, :].T)
        s_out[0:ROWS, cols] = high
        s_out[ROWS : 2 * ROWS, cols] = low

    @pl.when(holds_p)
    def _():
        wait_bytes(p_zb.at[pl.ds(0, DEPTH - 1)], pz_sem.at[1])
        total = p_zb[0]
        for j in range(1, DEPTH):
            total += p_zb[j]
        p_v[p_mine] = total
        send_plane(p_v.at[p_mine], p_sem)

    @pl.when(core == 1)
    def _():
        wait_bytes(zb.at[pl.ds(0, DEPTH - 1)], z_sem.at[1])
        total = zb[0]
        for j in range(1, DEPTH):
            total += zb[j]
        m_out[chip] = total
        send_plane(m_out.at[chip], m_sem)

    @pl.when(holds_p)
    def _():
        wait_bytes(p_v.at[pl.ds(0, P_TILES - 1)], p_sem.at[1])

    @pl.when(jnp.logical_not(holds_p))
    def _():
        wait_bytes(p_v, p_sem.at[1])

    first_out[...] = orthonormal_rows(p_v[...].reshape(RANK, ROWS))

    @pl.when(core == 0)
    def _():
        wait_bytes(m_out, m_sem.at[1])

    @pl.when(core == 1)
    def _():
        wait_bytes(m_out.at[pl.ds(0, CHIPS - 1)], m_sem.at[1])
        wait_bytes(zb.at[pl.ds(0, DEPTH - 1)], z_sem.at[0])
        wait_bytes(zb.at[pl.ds(0, PLANE - 1)], m_sem.at[0])

    swap.wait_send()

    @pl.when(holds_p)
    def _():
        wait_bytes(p_zb.at[pl.ds(0, DEPTH - 1)], pz_sem.at[0])
        wait_bytes(p_zb.at[pl.ds(0, PLANE - 1)], p_sem.at[0])
        wait_bytes(p_part.at[pl.ds(0, P_TILES - 1)], pt_sem.at[0])

    @pl.when(jnp.logical_not(holds_p))
    def _():
        wait_bytes(p_part, pt_sem.at[0])

    @pl.when(chip < OWNERS)
    def _():
        wait_bytes(ct.at[pl.ds(0, SLICE * (OWNERS - 1))], rs_sem.at[0])
        wait_bytes(st_v, st_sem.at[0])
        wait_bytes(st_v.at[pl.ds(0, COLS // 28 * 3)], st_sem.at[0])

        @pl.when(core == 0)
        def _():
            wait_bytes(part, tile_sem.at[0])

        @pl.when(core == 1)
        def _():
            wait_bytes(part.at[pl.ds(0, CHIPS - 1)], tile_sem.at[0])

    @pl.when(chip >= OWNERS)
    def _():
        wait_bytes(ct.at[pl.ds(0, HALF)], rs_sem.at[0])


def reduce_call(gradients, error_memory, qt_start):
    hbm = pl.BlockSpec(memory_space=pltpu.HBM)
    vmem = pl.BlockSpec(memory_space=pltpu.VMEM)
    pair = pltpu.SemaphoreType.DMA((2,))
    return pl.pallas_call(
        reduce_kernel,
        out_shape=(
            pltpu.VMEM((CHIPS, 8, ROWS), jnp.float32),
            pltpu.VMEM((2 * ROWS, COLS), jnp.bfloat16),
            pltpu.VMEM((ROWS, COLS), jnp.float32),
            pltpu.VMEM((RANK, ROWS), jnp.float32),
        ),
        in_specs=[hbm] * 3,
        out_specs=(vmem,) * 4,
        scratch_shapes=[
            pltpu.VMEM((ROWS, COLS), jnp.float32),
            pltpu.VMEM((ROWS, COLS), jnp.bfloat16),
            pltpu.VMEM((RANK, COLS), jnp.float32),
            pltpu.VMEM((COLS, ROWS), jnp.float32),
            pltpu.VMEM((HALF, ROWS), jnp.float32),
            pltpu.VMEM((CHIPS, SLICE, ROWS), jnp.float32),
            pltpu.VMEM((CHIPS, 8, ROWS), jnp.float32),
            pltpu.VMEM((SOURCES, 8, ROWS), jnp.float32),
            pltpu.VMEM((DEPTH, 8, ROWS), jnp.float32),
            pltpu.VMEM((COLS, ROWS), jnp.float32),
            pltpu.VMEM((P_TILES, 8, ROWS), jnp.float32),
            pltpu.VMEM((PLANE, 8, ROWS), jnp.float32),
            pltpu.VMEM((DEPTH, 8, ROWS), jnp.float32),
            pltpu.VMEM((P_TILES, 8, ROWS), jnp.float32),
            pltpu.SemaphoreType.DMA((3,)),
            pair, pair, pair, pair, pair, pair, pair, pair, pair,
            pltpu.SemaphoreType.REGULAR,
            pltpu.SemaphoreType.REGULAR,
        ],
        compiler_params=pltpu.CompilerParams(
            collective_id=0, has_side_effects=True, vmem_limit_bytes=VMEM_LIMIT
        ),
        name="plane_and_line_sums",
    )(gradients, error_memory, qt_start)


def orthonormal_rows(pt):
    gram = dot(pt, pt, 1, 1)
    high = RANK // 8
    gram = [gram[8 * t : 8 * t + 8] for t in range(high)]
    rows = [pt[8 * t : 8 * t + 8] for t in range(high)]
    pivots = [jnp.ones((8, ROWS), jnp.float32) for t in range(high)]
    sub = lax.broadcasted_iota(jnp.int32, (8, ROWS), 0)
    for first in range(0, RANK, BLOCK):
        more = first + BLOCK < RANK
        cols = [
            [jnp.broadcast_to(gram[t][:, first + j : first + j + 1], (8, ROWS)) for t in range(high)]
            for j in range(BLOCK)
        ]
        for j in range(BLOCK):
            at, s = divmod(first + j, 8)
            pivot = jnp.broadcast_to(cols[j][at][s : s + 1], (8, ROWS))
            inverse = 1.0 / pivot
            factor = [None] * high
            for t in range(at, high):
                factor[t] = cols[j][t] * inverse
            factor[at] = jnp.where(sub > s, factor[at], 0.0)
            for later in range(j + 1, BLOCK):
                entry = jnp.broadcast_to(cols[later][at][s : s + 1], (8, ROWS))
                for t in range(at, high):
                    cols[later][t] = cols[later][t] - factor[t] * entry
            row = jnp.broadcast_to(rows[at][s : s + 1], (8, ROWS))
            for t in range(at, high):
                rows[t] = rows[t] - factor[t] * row
            if more:
                line = jnp.broadcast_to(gram[at][s : s + 1], (8, RANK))
                for t in range(at, high):
                    gram[t] = gram[t] - factor[t][:, :RANK] * line
            pivots[at] = jnp.where(sub == s, pivot, pivots[at])
    return jnp.concatenate([rows[t] / jnp.sqrt(pivots[t]) for t in range(high)], axis=0)


def factor_kernel(m_ref, s_ref, c_ref, first_ref, p_hbm, qt_hbm, new_hbm, p_v, qt_v, new_v, store_sem):
    second = dot(first_ref[...], m_ref[...].reshape(ROWS, ROWS), 1, 0) * (1.0 / REPLICAS)
    pt = orthonormal_rows(second)
    left = pt.T
    z = lax.axis_index("tensor")
    p_v[0:ROWS, :] = left
    pair = p_v[pl.ds(pl.multiple_of(8 * lax.div(z, 2), 8), 8), :]
    p_v[ROWS : ROWS + 4, :] = jnp.where(lax.rem(z, 2) == 0, pair[0:4], pair[4:8])
    copies = [pltpu.make_async_copy(p_v.at[pl.ds(ROWS, 4)], p_hbm, store_sem.at[0])]
    copies[0].start()

    high, low = halves(pt)
    zero = jnp.zeros_like(low)
    rows = jnp.concatenate(
        [jnp.concatenate([high, high], axis=1), jnp.concatenate([low, zero], axis=1)], axis=0
    )
    high, low = halves(left)
    thrice = jnp.concatenate([high, high, low], axis=1)
    for b in range(len(STEPS) - 1):
        cols = slice(STEPS[b], STEPS[b + 1])
        both = jnp.dot(rows, s_ref[:, cols], preferred_element_type=jnp.float32)
        qt = (both[0:RANK] + both[RANK : 2 * RANK]) * (1.0 / REPLICAS)
        qt_v[:, cols] = qt
        high, low = halves(qt)
        product = jnp.dot(
            thrice, jnp.concatenate([high, low, high], axis=0), preferred_element_type=jnp.float32
        )
        new_v[:, cols] = (c_ref[:, cols] - product).astype(jnp.bfloat16)
        copies.append(pltpu.make_async_copy(new_v.at[:, cols], new_hbm.at[0, :, cols], store_sem.at[b + 2]))
        copies[-1].start()
    copies.append(pltpu.make_async_copy(qt_v, qt_hbm, store_sem.at[1]))
    copies[-1].start()
    for copy in copies:
        copy.wait()


def factor_call(tiles, split, corrected, first):
    hbm = pl.BlockSpec(memory_space=pltpu.HBM)
    vmem = pl.BlockSpec(memory_space=pltpu.VMEM)
    return pl.pallas_call(
        factor_kernel,
        out_shape=(
            jax.ShapeDtypeStruct((4, RANK), jnp.float32),
            jax.ShapeDtypeStruct((RANK, COLS), jnp.float32),
            jax.ShapeDtypeStruct((1, ROWS, COLS), jnp.bfloat16),
        ),
        in_specs=[vmem, vmem, vmem, vmem],
        out_specs=(hbm, hbm, hbm),
        scratch_shapes=[
            pltpu.VMEM((ROWS + 8, RANK), jnp.float32),
            pltpu.VMEM((RANK, COLS), jnp.float32),
            pltpu.VMEM((ROWS, COLS), jnp.bfloat16),
            pltpu.SemaphoreType.DMA((len(STEPS) + 1,)),
        ],
        compiler_params=pltpu.CompilerParams(vmem_limit_bytes=32 << 20),
        name="factors",
    )(tiles, split, corrected, first)


def local(gradients, error_memory, q_start):
    tiles, split, corrected, first = reduce_call(gradients, error_memory, q_start.T)
    p_rows, qt, new_error = factor_call(tiles, split, corrected, first)
    return p_rows, qt.T, new_error


def solution(mesh):
    in_specs = (P("dp", None, "tensor"), P("dp", None, "tensor"), P("tensor", None))
    out_specs = (P("tensor", None), P("tensor", None), P("dp", None, "tensor"))
    return jax.shard_map(local, mesh=mesh, in_specs=in_specs, out_specs=out_specs, check_vma=False)
```
